128 devices in a mesh: frame: 4 (over x_hi, core), patch: 32 (over x_lo, y, z).
Axes of the slice: x: 4 (x_hi: 2, x_lo: 2; x = x_hi * 2 + x_lo), y: 4, z: 4, core: 2. Of those that a mesh axis runs over, the one named last changes fastest.
Arguments:
- latent: bfloat16 [4, 64, 192, 640], P('frame', 'patch'), may hold values from -32 to 32
- gn_gain: float32 [640], replicated, may hold values from 0.1 to 1.9
- gn_bias: float32 [640], replicated, may hold values from -3 to 3
- conv_weight: bfloat16 [3, 3, 640, 640], replicated, may hold values from -0.15625 to 0.15625
- w_query: bfloat16 [640, 384], replicated, may hold values from -0.25 to 0.25
- w_kv: bfloat16 [640, 768], replicated, may hold values from -0.25 to 0.25
- w_out: bfloat16 [384, 640], replicated, may hold values from -0.3125 to 0.3125
- stale_kv: bfloat16 [4, 64, 192, 768], P('frame', 'patch'), may hold values from -190 to 190
- ln_gain: float32 [640], replicated, may hold values from 0.5 to 24
- ln_bias: float32 [640], replicated, may hold values from -3 to 3
- t_query: bfloat16 [640, 640], replicated, may hold values from -0.25 to 0.25
- t_kv: bfloat16 [640, 1280], replicated, may hold values from -0.25 to 0.25
- t_out: bfloat16 [640, 640], replicated, may hold values from -0.25 to 0.25
Outputs:
- block_out: float32 [4, 64, 192, 640], P('frame', 'patch')
- fresh_kv: bfloat16 [4, 64, 192, 768], P('frame', 'patch')
The draws below stay inside these ranges and needn't reach their ends.
All inputs are finite; a program needn't handle non-finite values.
Results may differ from the reference program's by a relative error of at most 0.04.
The reference program's roundings to bfloat16 on the way count: a program that leaves them out, or rounds other values in their place, can miss the bound.
Values may be sent and summed in bfloat16 or wider, within the bound.
A program may use at most 384 MiB of HBM per device.

```python
import math
import jax
import jax.numpy as jnp
from jax import lax

C = 640
THEADS = 8
GROUPS = 32
HEADS = 6
HEAD = 64
W = 192
ROWS_DEV = 2
THEAD = 80
HC = 384
NH = 64
FRAMES = 4
N_PATCH = 32


def draw_latent(key, part):
    key = jax.random.fold_in(key, 11)
    streams = jax.random.split(key, 3)
    full_shape = (FRAMES, NH, W, C)
    channel_scale = jnp.exp(jax.random.uniform(streams[0], (C,), jnp.float32, math.log(0.3), math.log(3.0)))
    offsets = jnp.clip(0.5 * jax.random.normal(streams[1], (C,), jnp.float32), -1.5, 1.5)
    position = jnp.arange(NH, dtype=jnp.float32) / max(NH - 1, 1)
    jitter = jnp.clip(jax.random.normal(streams[2], full_shape, jnp.float32), -4.0, 4.0)
    row_scale = 0.7 * 2.3 ** position
    return ((jitter * channel_scale + offsets) * row_scale[None, :, None, None]).astype(jnp.bfloat16)


def draw_stale_kv(key, part):
    key = jax.random.fold_in(key, 12)
    streams = jax.random.split(key, 1)
    inner = HEADS * HEAD
    full_shape = (FRAMES, NH * W, 2 * inner)
    column_scale = jnp.where(jnp.arange(2 * inner) < inner, 2.0, 1.0).astype(jnp.float32)
    result = jnp.clip(jax.random.normal(streams[0], full_shape, jnp.float32), -4.0, 4.0) * column_scale
    return result.reshape(FRAMES, NH, W, 2 * inner).astype(jnp.bfloat16)


def draw_ln_gain(key, part):
    key = jax.random.fold_in(key, 13)
    streams = jax.random.split(key, 2)
    result = jnp.exp(jax.random.uniform(streams[1], (C,), jnp.float32, math.log(0.5), math.log(2.0)))
    return result


def scatter_about(key, extent, width, most, kind=jnp.bfloat16):
    drawn = width * jax.random.normal(key, extent, jnp.float32)
    return jnp.clip(drawn, min=-most, max=most).astype(kind)


def setup_inputs(seed: int = 0) -> dict:
    keys = jax.random.split(jax.random.key(seed), 14)
    latent = draw_latent(jax.random.fold_in(keys[13], 71), 0)
    gn_gain = jnp.clip(1.0 + 0.18 * jax.random.normal(keys[1], (C,), jnp.float32), 0.1, 1.9)
    gn_bias = scatter_about(keys[2], (C,), 0.5, 3.0, jnp.float32)
    conv_weight = scatter_about(keys[3], (3, 3, C, C), (9 * C // 4) ** -0.5, 0.15625)
    w_query = scatter_about(keys[4], (C, HC), C ** -0.5, 0.25)
    w_kv = scatter_about(keys[5], (C, 2 * HC), C ** -0.5, 0.25)
    w_out = scatter_about(keys[6], (HC, C), HC ** -0.5, 0.3125)
    stale_kv = draw_stale_kv(jax.random.fold_in(keys[13], 71), 0)
    ln_gain = draw_ln_gain(jax.random.fold_in(keys[13], 71), 0)
    ln_bias = scatter_about(keys[9], (C,), 0.5, 3.0, jnp.float32)
    t_query = scatter_about(keys[10], (C, C), C ** -0.5, 0.25)
    t_kv = scatter_about(keys[11], (C, 2 * C), C ** -0.5, 0.25)
    t_out = scatter_about(keys[12], (C, C), C ** -0.5, 0.25)
    return {"latent": latent, "gn_gain": gn_gain, "gn_bias": gn_bias, "conv_weight": conv_weight, "w_query": w_query, "w_kv": w_kv, "w_out": w_out, "stale_kv": stale_kv, "ln_gain": ln_gain, "ln_bias": ln_bias, "t_query": t_query, "t_kv": t_kv, "t_out": t_out}


def position_code(frame_pos, channels):
    halves = jnp.arange(channels // 2, dtype=jnp.float32)
    freqs = jnp.exp(-math.log(10000.0) * 2.0 * halves / channels)
    angles = frame_pos[:, None] * freqs[None, :]
    return jnp.stack([jnp.sin(angles), jnp.cos(angles)], axis=-1).reshape(frame_pos.shape[0], channels)

def attend_block(query, keys_vals):
    inner = HEADS * HEAD
    pieces = []
    for head_index in range(HEADS):
        low = head_index * HEAD
        q_head = query[:, low:low + HEAD]
        k_head = keys_vals[:, low:low + HEAD]
        v_head = keys_vals[:, inner + low:inner + low + HEAD]
        scores = jnp.dot(q_head, k_head.T, preferred_element_type=jnp.float32) * HEAD ** (-0.5)
        shifted = jnp.exp(scores - lax.optimization_barrier(jnp.max(scores, axis=1, keepdims=True)))
        totals = lax.optimization_barrier(jnp.sum(shifted, axis=1, keepdims=True))
        weighted = jnp.dot(shifted.astype(jnp.bfloat16), v_head, preferred_element_type=jnp.float32)
        pieces.append(weighted / totals)
    return jnp.concatenate(pieces, axis=1).astype(jnp.bfloat16)

def reference(latent, gn_gain, gn_bias, conv_weight, w_query, w_kv, w_out, stale_kv, ln_gain, ln_bias, t_query, t_kv, t_out):
    frames, height, columns, channels = latent.shape
    per_group = channels // GROUPS
    cells = height * columns
    wide = latent.astype(jnp.float32).reshape(frames, cells, GROUPS, per_group)
    count = cells * per_group
    center = lax.optimization_barrier(jnp.sum(wide, axis=(1, 3))) / count
    variance = lax.optimization_barrier(jnp.sum(wide * wide, axis=(1, 3))) / count - center * center
    normed = (wide - center[:, None, :, None]) * lax.rsqrt(variance + 1e-05)[:, None, :, None]
    activ = normed.reshape(frames, height, columns, channels) * gn_gain + gn_bias
    hidden = jax.nn.silu(activ).astype(jnp.bfloat16)
    conv = lax.conv_general_dilated(hidden, conv_weight, (1, 1), ((1, 1), (1, 1)), dimension_numbers=('NHWC', 'HWIO', 'NHWC'), preferred_element_type=jnp.float32)
    resid = (latent.astype(jnp.float32) + conv).astype(jnp.bfloat16).reshape(frames * cells, channels)
    query = jnp.dot(resid, w_query, preferred_element_type=jnp.float32).astype(jnp.bfloat16)
    fresh = jnp.dot(resid, w_kv, preferred_element_type=jnp.float32).astype(jnp.bfloat16)
    span = ROWS_DEV * W
    width_kv = 2 * HEADS * HEAD
    starts = jnp.arange(N_PATCH, dtype=jnp.int32) * span
    zero_index = jnp.zeros((), jnp.int32)
    outputs = []
    for frame_index in range(frames):
        offset = frame_index * cells
        stale_frame = stale_kv[frame_index].reshape(cells, width_kv)
        q_frame = query[offset:offset + cells].reshape(N_PATCH, span, HEADS * HEAD)
        f_frame = fresh[offset:offset + cells].reshape(N_PATCH, span, width_kv)

        def one_patch(items, stale_frame=stale_frame):
            q_block, f_block, start = items
            keys_vals = lax.dynamic_update_slice(stale_frame, f_block, (start.astype(jnp.int32), zero_index))
            return attend_block(q_block, keys_vals)
        outputs.append(lax.map(one_patch, (q_frame, f_frame, starts)).reshape(cells, HEADS * HEAD))
    attn = jnp.concatenate(outputs, axis=0)
    mixed = (resid.astype(jnp.float32) + jnp.dot(attn, w_out, preferred_element_type=jnp.float32)).astype(jnp.bfloat16)
    mixed_wide = mixed.astype(jnp.float32).reshape(frames, cells, channels)
    lcenter = lax.optimization_barrier(jnp.mean(mixed_wide, axis=-1, keepdims=True))
    lvar = lax.optimization_barrier(jnp.mean(jnp.square(mixed_wide - lcenter), axis=-1, keepdims=True))
    codes = position_code(jnp.arange(frames).astype(jnp.float32), channels)
    units = ((mixed_wide - lcenter) * lax.rsqrt(lvar + 1e-05) * ln_gain + ln_bias + codes[:, None, :]).astype(jnp.bfloat16)
    units = units.reshape(frames * cells, channels)
    t_q = jnp.dot(units, t_query, preferred_element_type=jnp.float32).astype(jnp.bfloat16)
    t_k = jnp.dot(units, t_kv, preferred_element_type=jnp.float32).astype(jnp.bfloat16)
    t_q = lax.optimization_barrier(t_q).astype(jnp.float32).reshape(frames, cells, THEADS, THEAD)
    t_k = lax.optimization_barrier(t_k).astype(jnp.float32).reshape(frames, cells, 2, THEADS, THEAD)
    tscores = jnp.einsum('fthd,gthd->fthg', t_q, t_k[:, :, 0]) * THEAD ** (-0.5)
    texp = jnp.exp(tscores - lax.optimization_barrier(jnp.max(tscores, axis=-1, keepdims=True)))
    ttotals = lax.optimization_barrier(jnp.sum(texp, axis=-1))
    trounded = lax.optimization_barrier(texp.astype(jnp.bfloat16)).astype(jnp.float32)
    tweighted = jnp.einsum('fthg,gthd->fthd', trounded, t_k[:, :, 1]) / ttotals[..., None]
    tattn = tweighted.reshape(frames * cells, channels).astype(jnp.bfloat16)
    final = mixed.astype(jnp.float32) + jnp.dot(tattn, t_out, preferred_element_type=jnp.float32)
    return (final.reshape(frames, height, columns, channels), fresh.reshape(frames, height, columns, width_kv))
```

```python
import math

import jax
import jax.numpy as jnp
import numpy as np
from jax import lax
from jax.experimental import pallas as pl
from jax.experimental.pallas import tpu as pltpu
from jax.sharding import PartitionSpec as P

C = 640
THEADS = 8
GROUPS = 32
HEADS = 6
HEAD = 64
THEAD = 80
HC = 384
W = 192
T = 384
FRAMES = 4
QTR = 96
CHUNK = 1536
BF = jnp.bfloat16
F32 = jnp.float32
SCALE = HEAD ** (-0.5) * math.log2(math.e)
MESH = pl.DeviceIdType.MESH


def kernel(
    lat_h, stale_h, convw_h, wq_h, wkv_h, wout_h, tq_h, tkv_h, tout_h,
    gain_ref, bias_ref, lgain_ref, lbias_ref, code_ref, gmat_h, hsum_ref, hexp_ref,
    out_ref, fresh_h,
    lat, halo, convw, wqkv, wout, wt, tout, gmat, hcat, cacc, resid,
    stat1, stat2, qbuf, kv, acc, lbuf, mbuf, pout, pin, lout, lin,
    units, ubuf, tres, tbuf,
    lsem, hss, hrs, s1s, s1r, s2s, s2r, kss, krs, qss, qrs, pss, prs, lss, lrs, uss, urs, tss, trs,
):
    f = lax.axis_index("frame")
    p = lax.axis_index("patch")
    x = p // 16
    y = (p // 4) % 4
    z = p % 4

    def at(px, py, pz):
        return (f, px * 16 + py * 4 + pz)

    def remote(src, dst, ss, rs, dev):
        return pltpu.make_async_remote_copy(
            src_ref=src, dst_ref=dst, send_sem=ss, recv_sem=rs, device_id=dev, device_id_type=MESH
        )

    xy = [((x + dx) % 2, (y + dy) % 4) for dx, dy in ((0, 1), (0, 3), (1, 0), (0, 2), (1, 1), (1, 3), (1, 2))]
    xy_peers = [at(a, b, z) for a, b in xy]
    z_peers = {s: at(x, y, (z + s) % 4) for s in (1, 2, 3)}
    z_back = {s: at(x, y, (z + 4 - s) % 4) for s in (1, 2, 3)}
    up = (f, (p + 1) % 32)
    down = (f, (p + 31) % 32)
    f_ids = {1: f + 1 - 2 * (f % 2), 2: (f + 2) % 4, 3: 3 - f}
    f_peers = {d: (g, p) for d, g in f_ids.items()}

    loads = [
        pltpu.make_async_copy(lat_h, lat, lsem.at[0]),
        pltpu.make_async_copy(gmat_h, gmat, lsem.at[1]),
        pltpu.make_async_copy(convw_h, convw, lsem.at[2]),
        pltpu.make_async_copy(wq_h, wqkv.at[:, pl.ds(0, HC)], lsem.at[3]),
        pltpu.make_async_copy(wkv_h, wqkv.at[:, pl.ds(HC, 2 * HC)], lsem.at[4]),
        pltpu.make_async_copy(stale_h, kv.at[pl.ds(4 * T, T)], lsem.at[5]),
        pltpu.make_async_copy(wout_h, wout, lsem.at[6]),
        pltpu.make_async_copy(tq_h, wt.at[:, pl.ds(0, C)], lsem.at[7]),
        pltpu.make_async_copy(tkv_h, wt.at[:, pl.ds(C, 2 * C)], lsem.at[8]),
        pltpu.make_async_copy(tout_h, tout, lsem.at[9]),
    ]
    for c in loads:
        c.start()

    barrier = pltpu.get_barrier_semaphore()
    greet = xy_peers + list(z_peers.values()) + [up, down] + list(f_peers.values())
    for dev in greet:
        pl.semaphore_signal(barrier, inc=1, device_id=dev, device_id_type=MESH)

    row8 = lax.broadcasted_iota(jnp.int32, (8, C), 0)
    loads[0].wait()
    wide = lat[...].astype(F32)
    stat1[0, 0:1, :] = jnp.sum(wide, axis=0, keepdims=True)
    stat1[0, 1:2, :] = jnp.sum(wide * wide, axis=0, keepdims=True)
    pl.semaphore_wait(barrier, len(greet))

    sends = []
    st1 = [remote(stat1.at[0], stat1.at[1 + i], s1s.at[i], s1r.at[i], d) for i, d in enumerate(xy_peers)]
    for c in st1:
        c.start()
    halos = [
        remote(lat_h.at[pl.ds(W, W)], halo.at[0], hss.at[0], hrs.at[0], up),
        remote(lat_h.at[pl.ds(0, W)], halo.at[1], hss.at[1], hrs.at[1], down),
    ]
    for c in halos:
        c.start()
    spots = (1, 2, 3, 5)
    kvs = [
        remote(stale_h, kv.at[pl.ds(s * T, T)], kss.at[i], krs.at[i], xy_peers[i])
        for i, s in enumerate(spots)
    ]
    for c in kvs:
        c.start()

    for c in st1:
        c.wait_recv()
    stat2[0] = jnp.sum(stat1[...], axis=0)
    st2 = [remote(stat2.at[0], stat2.at[s], s2s.at[s - 1], s2r.at[s - 1], z_peers[s]) for s in (1, 3, 2)]
    for c in st2:
        c.start()
    loads[1].wait()
    for c in st2:
        c.wait_recv()
    total = jnp.sum(stat2[...], axis=0)
    total8 = jnp.where(row8 == 0, total[0:1], jnp.where(row8 == 1, total[1:2], 0.0))
    hi = total8.astype(BF).astype(F32)
    mid = (total8 - hi).astype(BF).astype(F32)
    low = total8 - hi - mid
    parts = jnp.concatenate([hi, mid, low, jnp.zeros((8, C), F32)], axis=0).astype(BF)
    summed = jnp.dot(parts, gmat[...], preferred_element_type=F32)
    summed = summed[0:8] + summed[8:16] + summed[16:24]
    count = float(32 * T * (C // GROUPS))
    center = summed[0:1] / count
    variance = summed[1:2] / count - center * center
    scale = lax.rsqrt(variance + 1e-05)
    gain = gain_ref[...]
    bias = bias_ref[...]

    wrow = lax.broadcasted_iota(jnp.int32, (W, C), 0)

    def hidden_row(block, r, keep):
        v = (block.astype(F32) - center) * scale * gain + bias
        h = v / (1.0 + jnp.exp(-v))
        if keep is not None:
            h = jnp.where(keep, h, 0.0)
        rows = pl.ds(r * W, W)
        hcat[rows, 0:C] = jnp.where(wrow == 0, 0.0, pltpu.roll(h, 1, 0)).astype(BF)
        hcat[rows, C : 2 * C] = h.astype(BF)
        hcat[rows, 2 * C : 3 * C] = jnp.where(wrow == W - 1, 0.0, pltpu.roll(h, W - 1, 0)).astype(BF)

    hidden_row(lat[0:W], 1, None)
    hidden_row(lat[W : 2 * W], 2, None)
    loads[2].wait()
    cacc[...] = jnp.dot(hcat[W : W + T], convw[1], preferred_element_type=F32)
    halos[0].wait_recv()
    halos[1].wait_recv()
    hidden_row(halo[0], 0, p > 0)
    hidden_row(halo[1], 3, p < 31)
    cacc[...] += jnp.dot(hcat[0:T], convw[0], preferred_element_type=F32)
    cacc[...] += jnp.dot(hcat[2 * W : 2 * W + T], convw[2], preferred_element_type=F32)
    resid[...] = (lat[...].astype(F32) + cacc[...]).astype(BF)

    loads[3].wait()
    loads[4].wait()
    qbuf[0] = (jnp.dot(resid[...], wqkv[:, 0:HC], preferred_element_type=F32) * SCALE).astype(BF)
    qs_send = [remote(qbuf.at[0], qbuf.at[s], qss.at[s - 1], qrs.at[s - 1], z_peers[s]) for s in (1, 3, 2)]
    for c in qs_send:
        c.start()
    kv[0:T] = jnp.dot(resid[...], wqkv[:, HC:], preferred_element_type=F32).astype(BF)
    fresh_copy = pltpu.make_async_copy(kv.at[pl.ds(0, T)], fresh_h, lsem.at[10])
    fresh_copy.start()

    for i in (0, 1, 2):
        kvs[i].wait_recv()
    fwd = [
        remote(kv.at[pl.ds(1 * T, T)], kv.at[pl.ds(6 * T, T)], kss.at[4], krs.at[4], xy_peers[2]),
        remote(kv.at[pl.ds(3 * T, T)], kv.at[pl.ds(8 * T, T)], kss.at[6], krs.at[6], xy_peers[3]),
        remote(kv.at[pl.ds(2 * T, T)], kv.at[pl.ds(7 * T, T)], kss.at[5], krs.at[5], xy_peers[2]),
    ]
    for c in fwd:
        c.start()
    loads[5].wait()

    lane = lax.broadcasted_iota(jnp.int32, (T, 128), 1)
    first = lane < HEAD
    ones = jnp.ones((CHUNK, 128), BF)

    def scores(qs, row0, h):
        q = qbuf[qs, :, (h // 2) * 128 : (h // 2) * 128 + 128]
        q = jnp.where(first if h % 2 == 0 else ~first, q, jnp.zeros_like(q))
        k = kv[pl.ds(row0, CHUNK), (h // 2) * 128 : (h // 2) * 128 + 128]
        return lax.dot_general(q, k, (((1,), (1,)), ((), ())), preferred_element_type=F32)

    def weigh(row0, h, prob):
        v = kv[pl.ds(row0, CHUNK), HC + (h // 2) * 128 : HC + (h // 2) * 128 + 128]
        return jnp.dot(prob, jnp.concatenate([v, ones], axis=1), preferred_element_type=F32)

    def pipeline(soft, done, qs, row0):
        ss, ps = {}, {}
        for i in range(HEADS + 2):
            if i < HEADS:
                ss[i] = scores(qs, row0, i)
            if 0 <= i - 1 < HEADS:
                ps[i - 1] = soft(ss.pop(i - 1), i - 1)
            if 0 <= i - 2 < HEADS:
                prob, extra = ps.pop(i - 2)
                done(i - 2, weigh(row0, i - 2, prob), extra)

    def first_chunk(t, carry):
        qs = t + (t // 2) * (5 - 2 * t)
        row0 = pl.multiple_of(jnp.where(t == 0, 0, T), T)

        @pl.when(t > 0)
        def _():
            remote(qbuf.at[0], qbuf.at[qs], qss.at[qs - 1], qrs.at[qs - 1], z_peers[1]).wait_recv()

        def soft(s, h):
            top = jnp.max(s, axis=1, keepdims=True)
            mbuf[qs, h] = jnp.broadcast_to(top, (T, 128))
            return jnp.exp2(s - top).astype(BF), None

        held = {}

        def done(h, r, _):
            lbuf[qs, h] = r[:, 128:]
            if h % 2 == 0:
                held[0] = r[:, :128]
            else:
                acc[qs, h // 2] = jnp.where(first, held.pop(0), r[:, :128])

        pipeline(soft, done, qs, row0)
        return carry

    lax.fori_loop(0, 4, first_chunk, 0)

    kvs[3].wait_recv()
    for c in fwd:
        c.wait_recv()

    def second_chunk(t, carry):
        qs = 3 - t
        row0 = 5 * T

        def soft(s, h):
            old = mbuf[qs, h]
            new = jnp.maximum(old, jnp.max(s, axis=1, keepdims=True))
            return jnp.exp2(s - new[:, :1]).astype(BF), (new, jnp.exp2(old - new))

        held = {}
        lses = jnp.zeros((T, 128), F32)

        def done(h, r, extra):
            nonlocal lses
            new, shrink = extra
            tot = lbuf[qs, h] * shrink + r[:, 128:]
            lses = jnp.where(lane == h, new + jnp.log2(tot), lses)
            o = acc[qs, h // 2] * shrink + r[:, :128]
            o = o / tot
            if h % 2 == 0:
                held[0] = o
            else:
                pout[qs, :, (h // 2) * 128 : (h // 2) * 128 + 128] = jnp.where(first, held.pop(0), o).astype(BF)

        pipeline(soft, done, qs, row0)
        lout[qs] = jnp.transpose(lses)[0:8]

        @pl.when(t < 3)
        def _():
            dev = at(x, y, (z + 1 + t) % 4)
            remote(pout.at[qs], pin.at[qs], pss.at[qs], prs.at[qs], dev).start()
            remote(lout.at[qs], lin.at[qs], lss.at[qs], lrs.at[qs], dev).start()

        return carry

    lax.fori_loop(0, 4, second_chunk, 0)

    backs = []
    for s in (3, 2, 1):
        backs.append(remote(pout.at[s], pin.at[s], pss.at[s], prs.at[s], z_back[s]))
        backs.append(remote(lout.at[s], lin.at[s], lss.at[s], lrs.at[s], z_back[s]))
    for c in backs:
        c.wait_recv()

    lse = [lout[0], lin[1], lin[2], lin[3]]
    top = jnp.maximum(jnp.maximum(lse[0], lse[1]), jnp.maximum(lse[2], lse[3]))
    ws = [jnp.exp2(v - top) for v in lse]
    tot = ws[0] + ws[1] + ws[2] + ws[3]
    ws = [jnp.transpose(v / tot) for v in ws]
    pairs = []
    for hp in range(HEADS // 2):
        cols = slice(hp * 128, hp * 128 + 128)
        o = None
        for s in range(4):
            part = (pout[0, :, cols] if s == 0 else pin[s, :, cols]).astype(F32)
            wgt = jnp.where(first, ws[s][:, 2 * hp : 2 * hp + 1], ws[s][:, 2 * hp + 1 : 2 * hp + 2])
            o = part * wgt if o is None else o + part * wgt
        pairs.append(o.astype(BF))
    attn = jnp.concatenate(pairs, axis=1)
    loads[6].wait()
    mixed = (resid[...].astype(F32) + jnp.dot(attn, wout[...], preferred_element_type=F32)).astype(BF)
    resid[...] = mixed
    mixed = mixed.astype(F32)
    mean = jnp.mean(mixed, axis=1, keepdims=True)
    dev = mixed - mean
    var = jnp.mean(dev * dev, axis=1, keepdims=True)
    units[...] = (
        dev * lax.rsqrt(var + 1e-05) * lgain_ref[...] + lbias_ref[...] + code_ref[pl.ds(f, 1), :]
    ).astype(BF)

    def quarter(g):
        return pl.ds(pl.multiple_of(g * QTR, QTR), QTR)

    us = [
        remote(units.at[quarter(f_ids[d])], ubuf.at[pl.ds(d * QTR, QTR)], uss.at[d - 1], urs.at[d - 1], f_peers[d])
        for d in (2, 3, 1)
    ]
    for c in us:
        c.start()
    ubuf[0:QTR] = units[quarter(f)]
    loads[7].wait()
    loads[8].wait()
    for c in us:
        c.wait_recv()
    tqkv = jnp.dot(ubuf[...], wt[...], preferred_element_type=F32).astype(BF).astype(F32)
    ts = []
    for a in range(FRAMES):
        tq = tqkv[a * QTR : (a + 1) * QTR, 0:C]
        his, los = [], []
        for b in range(FRAMES):
            prod = tq * tqkv[b * QTR : (b + 1) * QTR, C : 2 * C]
            phi = prod.astype(BF)
            his.append(phi)
            los.append((prod - phi.astype(F32)).astype(BF))
        lhs = jnp.concatenate([jnp.concatenate(his, axis=0), jnp.concatenate(los, axis=0)], axis=1)
        sc = jnp.dot(lhs, hsum_ref[...], preferred_element_type=F32) * THEAD ** (-0.5)
        sc = [sc[b * QTR : (b + 1) * QTR] for b in range(FRAMES)]
        top = jnp.maximum(jnp.maximum(sc[0], sc[1]), jnp.maximum(sc[2], sc[3]))
        es = [jnp.exp(v - top) for v in sc]
        rec = 1.0 / (es[0] + es[1] + es[2] + es[3])
        rhi = rec.astype(BF)
        rlo = (rec - rhi.astype(F32)).astype(BF)
        wide_rows = jnp.concatenate([e.astype(BF) for e in es] + [rhi, rlo], axis=0)
        ex = jnp.dot(wide_rows, hexp_ref[...], preferred_element_type=F32)
        o = None
        for b in range(FRAMES):
            term = ex[b * QTR : (b + 1) * QTR] * tqkv[b * QTR : (b + 1) * QTR, 2 * C : 3 * C]
            o = term if o is None else o + term
        o = o * (ex[4 * QTR : 5 * QTR] + ex[5 * QTR : 6 * QTR])
        if a == 0:
            tbuf[quarter(f), :] = o.astype(BF)
        else:
            tres[a] = o.astype(BF)
            ts.append(remote(tres.at[a], tbuf.at[quarter(f)], tss.at[a - 1], trs.at[a - 1], f_peers[a]))
            ts[-1].start()
    tback = [remote(tres.at[d], tbuf.at[quarter(f_ids[d])], tss.at[d - 1], trs.at[d - 1], f_peers[d]) for d in (1, 2, 3)]
    loads[9].wait()
    for c in tback:
        c.wait_recv()
    out_ref[...] = resid[...].astype(F32) + jnp.dot(tbuf[...], tout[...], preferred_element_type=F32)

    fresh_copy.wait()
    for c in st1 + halos + kvs + st2 + qs_send + fwd + backs + us + ts:
        c.wait_send()


def codes():
    halves = np.arange(C // 2, dtype=np.float64)
    freqs = np.exp(-math.log(10000.0) * 2.0 * halves / C)
    angles = np.arange(FRAMES)[:, None] * freqs[None, :]
    table = np.stack([np.sin(angles), np.cos(angles)], axis=-1).reshape(FRAMES, C)
    return np.concatenate([table, np.zeros((8 - FRAMES, C))]).astype(np.float32)


def shards(
    latent, gn_gain, gn_bias, conv_weight, w_query, w_kv, w_out, stale_kv, ln_gain, ln_bias, t_query, t_kv, t_out
):
    group = np.arange(C) // (C // GROUPS)
    gmat = jnp.asarray((group[:, None] == group[None, :]).astype(np.float32), BF)
    head = (np.arange(C)[:, None] // THEAD == np.arange(128)[None, :]).astype(np.float32)
    hsum = jnp.asarray(np.concatenate([head, head]), BF)
    hexp = jnp.asarray(head.T.copy(), BF)
    hbm = pl.BlockSpec(memory_space=pl.ANY)
    vmem = pl.BlockSpec(memory_space=pltpu.VMEM)
    dma = pltpu.SemaphoreType.DMA
    out, fresh = pl.pallas_call(
        kernel,
        out_shape=(jax.ShapeDtypeStruct((T, C), F32), jax.ShapeDtypeStruct((T, 2 * HC), BF)),
        in_specs=[hbm] * 9 + [vmem] * 5 + [hbm] + [vmem] * 2,
        out_specs=(vmem, hbm),
        scratch_shapes=[
            pltpu.VMEM((T, C), BF),
            pltpu.VMEM((2, W, C), BF),
            pltpu.VMEM((3, 3 * C, C), BF),
            pltpu.VMEM((C, 3 * HC), BF),
            pltpu.VMEM((HC, C), BF),
            pltpu.VMEM((C, 3 * C), BF),
            pltpu.VMEM((C, C), BF),
            pltpu.VMEM((C, C), BF),
            pltpu.VMEM((4 * W, 3 * C), BF),
            pltpu.VMEM((T, C), F32),
            pltpu.VMEM((T, C), BF),
            pltpu.VMEM((8, 2, C), F32),
            pltpu.VMEM((4, 2, C), F32),
            pltpu.VMEM((4, T, HC), BF),
            pltpu.VMEM((9 * T, 2 * HC), BF),
            pltpu.VMEM((4, HEADS // 2, T, 128), F32),
            pltpu.VMEM((4, HEADS, T, 128), F32),
            pltpu.VMEM((4, HEADS, T, 128), F32),
            pltpu.VMEM((4, T, HC), BF),
            pltpu.VMEM((4, T, HC), BF),
            pltpu.VMEM((4, 8, T), F32),
            pltpu.VMEM((4, 8, T), F32),
            pltpu.VMEM((T, C), BF),
            pltpu.VMEM((T, C), BF),
            pltpu.VMEM((4, QTR, C), BF),
            pltpu.VMEM((T, C), BF),
            dma((11,)), dma((2,)), dma((2,)), dma((7,)), dma((7,)), dma((3,)), dma((3,)),
            dma((7,)), dma((7,)), dma((3,)), dma((3,)), dma((4,)), dma((4,)), dma((4,)), dma((4,)),
            dma((3,)), dma((3,)), dma((3,)), dma((3,)),
        ],
        compiler_params=pltpu.CompilerParams(
            collective_id=0, has_side_effects=True, vmem_limit_bytes=63 * 2**20
        ),
    )(
        latent.reshape(T, C),
        stale_kv.reshape(T, 2 * HC),
        conv_weight.reshape(3, 3 * C, C),
        w_query,
        w_kv,
        w_out,
        t_query,
        t_kv,
        t_out,
        gn_gain.reshape(1, C),
        gn_bias.reshape(1, C),
        ln_gain.reshape(1, C),
        ln_bias.reshape(1, C),
        jnp.asarray(codes()),
        gmat,
        hsum,
        hexp,
    )
    return out.reshape(1, 2, W, C), fresh.reshape(1, 2, W, 2 * HC)


def solution(mesh):
    sharded = P("frame", "patch", None, None)
    placed = (sharded,) + (P(),) * 6 + (sharded,) + (P(),) * 5
    return jax.shard_map(
        shards, mesh=mesh, in_specs=placed, out_specs=(sharded, sharded), check_vma=False
    )
```

```python
import math

import jax
import jax.numpy as jnp
import numpy as np
from jax import lax
from jax.experimental import pallas as pl
from jax.experimental.pallas import tpu as pltpu
from jax.sharding import PartitionSpec as P

C = 640
THEADS = 8
GROUPS = 32
HEADS = 6
HEAD = 64
THEAD = 80
HC = 384
W = 192
T = 384
FRAMES = 4
HALF = 192
QTR = 48
LSE = 256
CHUNK = 1536
BF = jnp.bfloat16
F32 = jnp.float32
SCALE = HEAD ** (-0.5) * math.log2(math.e)
MESH = pl.DeviceIdType.MESH


def kernel(
    lat_h, stale_h, convw_h, wq_h, wkv_h, wout_h, tq_h, tkv_h, tout_h,
    gain_ref, bias_ref, lgain_ref, lbias_ref, code_ref, gmat_h, hsum_ref, hexp_ref,
    out_ref, fresh_h,
    lat, halo, convw, wqkv, wout, wt, tout, gmat, hcat, cacc, resid,
    stat1, stat2, qbuf, kv, acc, lbuf, mbuf, pout, pin, lout, lin,
    units, ubuf, tres, tbuf,
    lsem, hss, hrs, s1s, s1r, s2s, s2r, kss, krs, qss, qrs, pss, prs, lss, lrs, uss, urs, tss, trs,
):
    f = lax.axis_index("frame")
    p = lax.axis_index("patch")
    x = p // 16
    y = (p // 4) % 4
    z = p % 4

    def at(px, py, pz):
        return (f, px * 16 + py * 4 + pz)

    def remote(src, dst, ss, rs, dev):
        return pltpu.make_async_remote_copy(
            src_ref=src, dst_ref=dst, send_sem=ss, recv_sem=rs, device_id=dev, device_id_type=MESH
        )

    xy = [((x + dx) % 2, (y + dy) % 4) for dx, dy in ((0, 1), (0, 3), (1, 0), (0, 2), (1, 1), (1, 3), (1, 2))]
    xy_peers = [at(a, b, z) for a, b in xy]
    y_up, y_down, x_other = xy_peers[:3]
    z_peers = {s: at(x, y, (z + s) % 4) for s in (1, 2, 3)}
    z_back = {s: at(x, y, (z + 4 - s) % 4) for s in (1, 2, 3)}
    up = (f, (p + 1) % 32)
    down = (f, (p + 31) % 32)
    f_ids = {0: f, 1: f + 1 - 2 * (f % 2), 2: (f + 2) % 4, 3: 3 - f}
    f_peers = {d: (f_ids[d], p) for d in (1, 2, 3)}

    loads = [
        pltpu.make_async_copy(lat_h, lat, lsem.at[0]),
        pltpu.make_async_copy(gmat_h, gmat, lsem.at[1]),
        pltpu.make_async_copy(convw_h, convw, lsem.at[2]),
        pltpu.make_async_copy(wq_h, wqkv.at[:, pl.ds(0, HC)], lsem.at[3]),
        pltpu.make_async_copy(wkv_h, wqkv.at[:, pl.ds(HC, 2 * HC)], lsem.at[4]),
        pltpu.make_async_copy(stale_h, kv.at[pl.ds(4 * T, T)], lsem.at[5]),
        pltpu.make_async_copy(wout_h, wout, lsem.at[6]),
        pltpu.make_async_copy(tq_h, wt.at[:, pl.ds(0, C)], lsem.at[7]),
        pltpu.make_async_copy(tkv_h, wt.at[:, pl.ds(C, 2 * C)], lsem.at[8]),
        pltpu.make_async_copy(tout_h, tout, lsem.at[9]),
    ]
    for c in loads:
        c.start()

    barrier = pltpu.get_barrier_semaphore()
    greet = xy_peers + list(z_peers.values()) + [up, down] + list(f_peers.values())
    for dev in greet:
        pl.semaphore_signal(barrier, inc=1, device_id=dev, device_id_type=MESH)

    row8 = lax.broadcasted_iota(jnp.int32, (8, C), 0)
    loads[0].wait()
    wide = lat[...].astype(F32)
    stat1[0, 0:1, :] = jnp.sum(wide, axis=0, keepdims=True)
    stat1[0, 1:2, :] = jnp.sum(wide * wide, axis=0, keepdims=True)
    pl.semaphore_wait(barrier, len(greet))

    st1 = [remote(stat1.at[0], stat1.at[1 + i], s1s.at[i], s1r.at[i], d) for i, d in enumerate(xy_peers)]
    for c in st1:
        c.start()
    halos = [
        remote(lat_h.at[pl.ds(W, W)], halo.at[0], hss.at[0], hrs.at[0], up),
        remote(lat_h.at[pl.ds(0, W)], halo.at[1], hss.at[1], hrs.at[1], down),
    ]
    for c in halos:
        c.start()

    def block(s, low=0, rows=T):
        return kv.at[pl.ds(s * T + low, rows)]

    def passed(i, src, dst, low, rows, dev):
        return remote(block(src, low, rows), block(dst, low, rows), kss.at[i], krs.at[i], dev)

    wave1 = [
        remote(stale_h, block(1), kss.at[0], krs.at[0], y_up),
        remote(stale_h, block(2), kss.at[1], krs.at[1], y_down),
        remote(stale_h, block(3), kss.at[2], krs.at[2], x_other),
    ]
    wave2 = [
        passed(3, 1, 6, 128, 64, x_other),
        passed(5, 3, 6, 0, 128, y_up),
        passed(6, 3, 7, 256, 128, y_down),
        passed(4, 2, 7, 192, 64, x_other),
        passed(7, 1, 5, 0, 192, y_up),
        passed(8, 2, 5, 192, 192, y_down),
        passed(9, 1, 6, 192, 192, x_other),
        passed(10, 2, 7, 0, 192, x_other),
    ]
    wave3 = [
        passed(11, 6, 8, 0, 192, y_up),
        passed(12, 7, 8, 192, 192, y_down),
    ]
    for c in wave1:
        c.start()

    for c in st1:
        c.wait_recv()
    stat2[0] = jnp.sum(stat1[...], axis=0)
    st2 = [remote(stat2.at[0], stat2.at[s], s2s.at[s - 1], s2r.at[s - 1], z_peers[s]) for s in (1, 3, 2)]
    for c in st2:
        c.start()
    loads[1].wait()
    for c in st2:
        c.wait_recv()
    total = jnp.sum(stat2[...], axis=0)
    total8 = jnp.where(row8 == 0, total[0:1], jnp.where(row8 == 1, total[1:2], 0.0))
    hi = total8.astype(BF).astype(F32)
    mid = (total8 - hi).astype(BF).astype(F32)
    low = total8 - hi - mid
    parts = jnp.concatenate([hi, mid, low, jnp.zeros((8, C), F32)], axis=0).astype(BF)
    summed = jnp.dot(parts, gmat[...], preferred_element_type=F32)
    summed = summed[0:8] + summed[8:16] + summed[16:24]
    count = float(32 * T * (C // GROUPS))
    center = summed[0:1] / count
    variance = summed[1:2] / count - center * center
    scale = lax.rsqrt(variance + 1e-05)
    gain = gain_ref[...].reshape(1, C)
    bias = bias_ref[...].reshape(1, C)

    wrow = lax.broadcasted_iota(jnp.int32, (W, C), 0)

    def hidden_row(block, r, keep):
        v = (block.astype(F32) - center) * scale * gain + bias
        h = v / (1.0 + jnp.exp(-v))
        if keep is not None:
            h = jnp.where(keep, h, 0.0)
        rows = pl.ds(r * W, W)
        hcat[rows, 0:C] = jnp.where(wrow == 0, 0.0, pltpu.roll(h, 1, 0)).astype(BF)
        hcat[rows, C : 2 * C] = h.astype(BF)
        hcat[rows, 2 * C : 3 * C] = jnp.where(wrow == W - 1, 0.0, pltpu.roll(h, W - 1, 0)).astype(BF)

    hidden_row(lat[0:W], 1, None)
    hidden_row(lat[W : 2 * W], 2, None)
    loads[2].wait()
    cacc[...] = jnp.dot(hcat[W : W + T], convw[1], preferred_element_type=F32)
    halos[0].wait_recv()
    halos[1].wait_recv()
    hidden_row(halo[0], 0, p > 0)
    hidden_row(halo[1], 3, p < 31)
    cacc[...] += jnp.dot(hcat[0:T], convw[0], preferred_element_type=F32)
    cacc[...] += jnp.dot(hcat[2 * W : 2 * W + T], convw[2], preferred_element_type=F32)
    resid[...] = (lat[...].astype(F32) + cacc[...]).astype(BF)

    def half(h):
        return pl.ds(pl.multiple_of(h * HALF, HALF), HALF)

    def q_copy(s, h, dev, src=0):
        i = (s - 1) * 2 + h
        return remote(qbuf.at[src, half(h)], qbuf.at[s, half(h)], qss.at[i], qrs.at[i], dev)

    loads[3].wait()
    loads[4].wait()
    qbuf[0] = (jnp.dot(resid[...], wqkv[:, 0:HC], preferred_element_type=F32) * SCALE).astype(BF)
    q_sends = [q_copy(s, h, z_peers[s]) for h in (0, 1) for s in (1, 3)]
    for c in q_sends:
        c.start()
    kv[0:T] = jnp.dot(resid[...], wqkv[:, HC:], preferred_element_type=F32).astype(BF)
    fresh_copy = pltpu.make_async_copy(kv.at[pl.ds(0, T)], fresh_h, lsem.at[10])
    fresh_copy.start()

    for c in wave1:
        c.wait_recv()
    for c in wave2:
        c.start()
    loads[5].wait()

    lane = lax.broadcasted_iota(jnp.int32, (HALF, 128), 1)
    first = lane < HEAD
    ones = jnp.ones((CHUNK, 128), BF)

    def scores(qs, rows, row0, h):
        q = qbuf[qs, rows, (h // 2) * 128 : (h // 2) * 128 + 128]
        q = jnp.where(first if h % 2 == 0 else ~first, q, jnp.zeros_like(q))
        k = kv[pl.ds(row0, CHUNK), (h // 2) * 128 : (h // 2) * 128 + 128]
        return lax.dot_general(q, k, (((1,), (1,)), ((), ())), preferred_element_type=F32)

    def weigh(row0, h, prob):
        v = kv[pl.ds(row0, CHUNK), HC + (h // 2) * 128 : HC + (h // 2) * 128 + 128]
        return jnp.dot(prob, jnp.concatenate([v, ones], axis=1), preferred_element_type=F32)

    def pipeline(soft, done, qs, rows, row0):
        ss, ps = {}, {}
        for i in range(HEADS + 2):
            if i < HEADS:
                ss[i] = scores(qs, rows, row0, i)
            if 0 <= i - 1 < HEADS:
                ps[i - 1] = soft(ss.pop(i - 1), i - 1)
            if 0 <= i - 2 < HEADS:
                prob, extra = ps.pop(i - 2)
                done(i - 2, weigh(row0, i - 2, prob), extra)

    def first_chunk(t, carry):
        qs = jnp.where(t < 2, 0, jnp.where(t < 6, 1 + 2 * (t % 2), 2))
        hh = jnp.where(t < 2, t, jnp.where(t < 6, (t - 2) // 2, t - 6))
        rows = half(hh)
        row0 = pl.multiple_of(jnp.where(t < 2, 0, T), T)

        @pl.when(t >= 2)
        def _():
            q_copy(qs, hh, z_peers[1]).wait_recv()

        @pl.when((t == 2) | (t == 4))
        def _():
            q_copy(2, hh, z_peers[1], src=1).start()

        @pl.when(t == 4)
        def _():
            for c in wave2[:4]:
                c.wait_recv()
            for c in wave3:
                c.start()

        def soft(s, h):
            top = jnp.max(s, axis=1, keepdims=True)
            mbuf[qs, h, rows] = jnp.broadcast_to(top, (HALF, 128))
            return jnp.exp2(s - top).astype(BF), None

        held = {}

        def done(h, r, _):
            lbuf[qs, h, rows] = r[:, 128:]
            if h % 2 == 0:
                held[0] = r[:, :128]
            else:
                acc[qs, h // 2, rows] = jnp.where(first, held.pop(0), r[:, :128])

        pipeline(soft, done, qs, rows, row0)
        return carry

    lax.fori_loop(0, 8, first_chunk, 0)

    for c in wave2[4:] + wave3:
        c.wait_recv()

    def part_copies(s, h, dev):
        i = s * 2 + h
        return [
            remote(pout.at[s, half(h)], pin.at[s, half(h)], pss.at[i], prs.at[i], dev),
            remote(lout.at[s, h], lin.at[s, h], lss.at[i], lrs.at[i], dev),
        ]

    def quarter(h, g):
        return pl.ds(pl.multiple_of(h * HALF + g * QTR, QTR), QTR)

    def unit_copy(d, h):
        i = (d - 1) * 2 + h
        return remote(units.at[quarter(h, f_ids[d])], ubuf.at[quarter(h, d)], uss.at[i], urs.at[i], f_peers[d])

    def back_copy(d, h, owner):
        i = (d - 1) * 2 + h
        return remote(tres.at[h, d], tbuf.at[quarter(h, owner)], tss.at[i], trs.at[i], f_peers[d])

    def combine(h):
        rows = half(h)
        for s in (3, 2, 1):
            for c in part_copies(s, h, z_back[s]):
                c.wait_recv()
        lse = [lout[0, h], lin[1, h], lin[2, h], lin[3, h]]
        top = jnp.maximum(jnp.maximum(lse[0], lse[1]), jnp.maximum(lse[2], lse[3]))
        ws = [jnp.exp2(v - top) for v in lse]
        tot = ws[0] + ws[1] + ws[2] + ws[3]
        ws = [jnp.transpose(v / tot)[0:HALF] for v in ws]
        pairs = []
        for hp in range(HEADS // 2):
            cols = slice(hp * 128, hp * 128 + 128)
            o = None
            for s in range(4):
                part = (pout[0, rows, cols] if s == 0 else pin[s, rows, cols]).astype(F32)
                wgt = jnp.where(first, ws[s][:, 2 * hp : 2 * hp + 1], ws[s][:, 2 * hp + 1 : 2 * hp + 2])
                o = part * wgt if o is None else o + part * wgt
            pairs.append(o.astype(BF))
        attn = jnp.concatenate(pairs, axis=1)
        mixed = (resid[rows].astype(F32) + jnp.dot(attn, wout[...], preferred_element_type=F32)).astype(BF)
        resid[rows] = mixed
        mixed = mixed.astype(F32)
        mean = jnp.mean(mixed, axis=1, keepdims=True)
        dev = mixed - mean
        var = jnp.mean(dev * dev, axis=1, keepdims=True)
        lgain = lgain_ref[...].reshape(1, C)
        lbias = lbias_ref[...].reshape(1, C)
        units[rows] = (dev * lax.rsqrt(var + 1e-05) * lgain + lbias + code_ref[pl.ds(f, 1), :]).astype(BF)
        for d in (2, 3, 1):
            unit_copy(d, h).start()
        ubuf[quarter(h, 0)] = units[quarter(h, f)]

    def temporal(h):
        for d in (1, 2, 3):
            unit_copy(d, h).wait_recv()
        tqkv = jnp.dot(ubuf[half(h)], wt[...], preferred_element_type=F32).astype(BF).astype(F32)
        for a in (2, 3, 1, 0):
            tq = tqkv[a * QTR : (a + 1) * QTR, 0:C]
            his, los = [], []
            for b in range(FRAMES):
                prod = tq * tqkv[b * QTR : (b + 1) * QTR, C : 2 * C]
                phi = prod.astype(BF)
                his.append(phi)
                los.append((prod - phi.astype(F32)).astype(BF))
            lhs = jnp.concatenate([jnp.concatenate(his, axis=0), jnp.concatenate(los, axis=0)], axis=1)
            sc = jnp.dot(lhs, hsum_ref[...], preferred_element_type=F32) * THEAD ** (-0.5)
            sc = [sc[b * QTR : (b + 1) * QTR] for b in range(FRAMES)]
            top = jnp.maximum(jnp.maximum(sc[0], sc[1]), jnp.maximum(sc[2], sc[3]))
            es = [jnp.exp(v - top) for v in sc]
            rec = 1.0 / (es[0] + es[1] + es[2] + es[3])
            rhi = rec.astype(BF)
            rlo = (rec - rhi.astype(F32)).astype(BF)
            wide_rows = jnp.concatenate([e.astype(BF) for e in es] + [rhi, rlo], axis=0)
            ex = jnp.dot(wide_rows, hexp_ref[...], preferred_element_type=F32)
            o = None
            for b in range(FRAMES):
                term = ex[b * QTR : (b + 1) * QTR] * tqkv[b * QTR : (b + 1) * QTR, 2 * C : 3 * C]
                o = term if o is None else o + term
            o = (o * (ex[4 * QTR : 5 * QTR] + ex[5 * QTR : 6 * QTR])).astype(BF)
            if a == 0:
                tbuf[quarter(h, f)] = o
            else:
                tres[h, a] = o
                back_copy(a, h, f).start()

    def finish(h):
        for d in (1, 2, 3):
            back_copy(d, h, f_ids[d]).wait_recv()
        rows = half(h)
        out_ref[rows] = resid[rows].astype(F32) + jnp.dot(tbuf[rows], tout[...], preferred_element_type=F32)

    for i in (6, 7, 8, 9):
        loads[i].wait()

    def second_chunk(t, carry):
        hh = t // 4
        qs = 3 - t % 4
        rows = half(hh)
        row0 = 5 * T

        def soft(s, h):
            old = mbuf[qs, h, rows]
            new = jnp.maximum(old, jnp.max(s, axis=1, keepdims=True))
            return jnp.exp2(s - new[:, :1]).astype(BF), (new, jnp.exp2(old - new))

        held = {}
        lses = jnp.zeros((HALF, 128), F32)

        def done(h, r, extra):
            nonlocal lses
            new, shrink = extra
            tot = lbuf[qs, h, rows] * shrink + r[:, 128:]
            lses = jnp.where(lane == h, new + jnp.log2(tot), lses)
            o = acc[qs, h // 2, rows] * shrink + r[:, :128]
            o = o / tot
            if h % 2 == 0:
                held[0] = o
            else:
                pout[qs, rows, (h // 2) * 128 : (h // 2) * 128 + 128] = jnp.where(first, held.pop(0), o).astype(BF)

        pipeline(soft, done, qs, rows, row0)
        lses = jnp.concatenate([lses, jnp.zeros((LSE - HALF, 128), F32)], axis=0)
        lout[qs, hh] = jnp.transpose(lses)[0:8]

        @pl.when(qs > 0)
        def _():
            for c in part_copies(qs, hh, at(x, y, (z + 4 - qs) % 4)):
                c.start()

        @pl.when(t == 4)
        def _():
            combine(0)

        @pl.when(t == 6)
        def _():
            temporal(0)

        return carry

    lax.fori_loop(0, 8, second_chunk, 0)
    combine(1)
    temporal(1)
    finish(0)
    finish(1)

    fresh_copy.wait()
    for c in st1 + halos + wave1 + wave2 + wave3 + st2 + q_sends:
        c.wait_send()
    for h in (0, 1):
        q_copy(2, h, z_peers[1], src=1).wait_send()
        for s in (1, 2, 3):
            for c in part_copies(s, h, z_back[s]):
                c.wait_send()
            unit_copy(s, h).wait_send()
            back_copy(s, h, f).wait_send()


def codes():
    halves = np.arange(C // 2, dtype=np.float64)
    freqs = np.exp(-math.log(10000.0) * 2.0 * halves / C)
    angles = np.arange(FRAMES)[:, None] * freqs[None, :]
    table = np.stack([np.sin(angles), np.cos(angles)], axis=-1).reshape(FRAMES, C)
    return np.concatenate([table, np.zeros((8 - FRAMES, C))]).astype(np.float32)


def shards(
    latent, gn_gain, gn_bias, conv_weight, w_query, w_kv, w_out, stale_kv, ln_gain, ln_bias, t_query, t_kv, t_out
):
    group = np.arange(C) // (C // GROUPS)
    gmat = jnp.asarray((group[:, None] == group[None, :]).astype(np.float32), BF)
    head = (np.arange(C)[:, None] // THEAD == np.arange(128)[None, :]).astype(np.float32)
    hsum = jnp.asarray(np.concatenate([head, head]), BF)
    hexp = jnp.asarray(head.T.copy(), BF)
    hbm = pl.BlockSpec(memory_space=pl.ANY)
    vmem = pl.BlockSpec(memory_space=pltpu.VMEM)
    dma = pltpu.SemaphoreType.DMA
    out, fresh = pl.pallas_call(
        kernel,
        out_shape=(jax.ShapeDtypeStruct((T, C), F32), jax.ShapeDtypeStruct((T, 2 * HC), BF)),
        in_specs=[hbm] * 9 + [vmem] * 5 + [hbm] + [vmem] * 2,
        out_specs=(vmem, hbm),
        scratch_shapes=[
            pltpu.VMEM((T, C), BF),
            pltpu.VMEM((2, W, C), BF),
            pltpu.VMEM((3, 3 * C, C), BF),
            pltpu.VMEM((C, 3 * HC), BF),
            pltpu.VMEM((HC, C), BF),
            pltpu.VMEM((C, 3 * C), BF),
            pltpu.VMEM((C, C), BF),
            pltpu.VMEM((C, C), BF),
            pltpu.VMEM((4 * W, 3 * C), BF),
            pltpu.VMEM((T, C), F32),
            pltpu.VMEM((T, C), BF),
            pltpu.VMEM((8, 2, C), F32),
            pltpu.VMEM((4, 2, C), F32),
            pltpu.VMEM((4, T, HC), BF),
            pltpu.VMEM((9 * T, 2 * HC), BF),
            pltpu.VMEM((4, HEADS // 2, T, 128), F32),
            pltpu.VMEM((4, HEADS, T, 128), F32),
            pltpu.VMEM((4, HEADS, T, 128), F32),
            pltpu.VMEM((4, T, HC), BF),
            pltpu.VMEM((4, T, HC), BF),
            pltpu.VMEM((4, 2, 8, LSE), F32),
            pltpu.VMEM((4, 2, 8, LSE), F32),
            pltpu.VMEM((T, C), BF),
            pltpu.VMEM((T, C), BF),
            pltpu.VMEM((2, 4, QTR, C), BF),
            pltpu.VMEM((T, C), BF),
            dma((11,)), dma((2,)), dma((2,)), dma((7,)), dma((7,)), dma((3,)), dma((3,)),
            dma((13,)), dma((13,)), dma((6,)), dma((6,)), dma((8,)), dma((8,)), dma((8,)), dma((8,)),
            dma((6,)), dma((6,)), dma((6,)), dma((6,)),
        ],
        compiler_params=pltpu.CompilerParams(
            collective_id=0, has_side_effects=True, vmem_limit_bytes=63 * 2**20
        ),
    )(
        latent.reshape(T, C),
        stale_kv.reshape(T, 2 * HC),
        conv_weight.reshape(3, 3 * C, C),
        w_query,
        w_kv,
        w_out,
        t_query,
        t_kv,
        t_out,
        gn_gain,
        gn_bias,
        ln_gain,
        ln_bias,
        jnp.asarray(codes()),
        gmat,
        hsum,
        hexp,
    )
    return out.reshape(1, 2, W, C), fresh.reshape(1, 2, W, 2 * HC)


def solution(mesh):
    sharded = P("frame", "patch", None, None)
    placed = (sharded,) + (P(),) * 6 + (sharded,) + (P(),) * 5
    return jax.shard_map(
        shards, mesh=mesh, in_specs=placed, out_specs=(sharded, sharded), check_vma=False
    )
```

```python
import math

import jax
import jax.numpy as jnp
import numpy as np
from jax import lax
from jax.experimental import pallas as pl
from jax.experimental.pallas import tpu as pltpu
from jax.sharding import PartitionSpec as P

C = 640
THEADS = 8
GROUPS = 32
HEADS = 6
HEAD = 64
THEAD = 80
HC = 384
W = 192
T = 384
FRAMES = 4
HALF = 192
QTR = 48
LSE = 256
PARTS = 4
CHUNK = 1536
BF = jnp.bfloat16
F32 = jnp.float32
SCALE = HEAD ** (-0.5) * math.log2(math.e)
MESH = pl.DeviceIdType.MESH


def kernel(
    lat_h, stale_h, convw_h, wq_h, wkv_h, wout_h, tq_h, tkv_h, tout_h,
    gain_ref, bias_ref, lgain_ref, lbias_ref, code_ref, gmat_h, hsum_h, hexp_h,
    out_ref, fresh_h,
    lat, halo, convw, wqkv, wout, wt, tout, gmat, hcat, cacc, resid,
    stat1, stat2, qbuf, kv, acc, lbuf, mbuf, pout, pin, lout, lin,
    units, ubuf, tres, tbuf, hsum_ref, hexp_ref,
    lsem, hss, hrs, s1s, s1r, s2s, s2r, kss, krs, qss, qrs, pss, prs, lss, lrs, uss, urs, tss, trs,
):
    f = lax.axis_index("frame")
    p = lax.axis_index("patch")
    x = p // 16
    y = (p // 4) % 4
    z = p % 4

    def at(px, py, pz):
        return (f, px * 16 + py * 4 + pz)

    def remote(src, dst, ss, rs, dev):
        return pltpu.make_async_remote_copy(
            src_ref=src, dst_ref=dst, send_sem=ss, recv_sem=rs, device_id=dev, device_id_type=MESH
        )

    xy = [((x + dx) % 2, (y + dy) % 4) for dx, dy in ((0, 1), (0, 3), (1, 0), (0, 2), (1, 1), (1, 3), (1, 2))]
    xy_peers = [at(a, b, z) for a, b in xy]
    y_up, y_down, x_other = xy_peers[:3]
    z_peers = {s: at(x, y, (z + s) % 4) for s in (1, 2, 3)}
    z_back = {s: at(x, y, (z + 4 - s) % 4) for s in (1, 2, 3)}
    up = (f, (p + 1) % 32)
    down = (f, (p + 31) % 32)
    f_ids = {0: f, 1: f + 1 - 2 * (f % 2), 2: (f + 2) % 4, 3: 3 - f}
    f_peers = {d: (f_ids[d], p) for d in (1, 2, 3)}

    loads = [
        pltpu.make_async_copy(lat_h, lat, lsem.at[0]),
        pltpu.make_async_copy(gmat_h, gmat, lsem.at[1]),
        pltpu.make_async_copy(convw_h, convw, lsem.at[2]),
        pltpu.make_async_copy(wq_h, wqkv.at[:, pl.ds(0, HC)], lsem.at[3]),
        pltpu.make_async_copy(wkv_h, wqkv.at[:, pl.ds(HC, 2 * HC)], lsem.at[4]),
        pltpu.make_async_copy(stale_h, kv.at[pl.ds(4 * T, T)], lsem.at[5]),
        pltpu.make_async_copy(wout_h, wout, lsem.at[6]),
        pltpu.make_async_copy(tq_h, wt.at[:, pl.ds(0, C)], lsem.at[7]),
        pltpu.make_async_copy(tkv_h, wt.at[:, pl.ds(C, 2 * C)], lsem.at[8]),
        pltpu.make_async_copy(tout_h, tout, lsem.at[9]),
        pltpu.make_async_copy(hsum_h, hsum_ref, lsem.at[11]),
        pltpu.make_async_copy(hexp_h, hexp_ref, lsem.at[12]),
    ]
    for c in loads:
        c.start()

    barrier = pltpu.get_barrier_semaphore()
    greet = xy_peers + list(z_peers.values()) + [up, down] + list(f_peers.values())
    for dev in greet:
        pl.semaphore_signal(barrier, inc=1, device_id=dev, device_id_type=MESH)

    row8 = lax.broadcasted_iota(jnp.int32, (8, C), 0)
    loads[0].wait()
    wide = lat[...].astype(F32)
    stat1[0, 0:1, :] = jnp.sum(wide, axis=0, keepdims=True)
    stat1[0, 1:2, :] = jnp.sum(wide * wide, axis=0, keepdims=True)
    pl.semaphore_wait(barrier, len(greet))

    st1 = [remote(stat1.at[0], stat1.at[1 + i], s1s.at[i], s1r.at[i], d) for i, d in enumerate(xy_peers)]
    for c in st1:
        c.start()
    halos = [
        remote(lat_h.at[pl.ds(W, W)], halo.at[0], hss.at[0], hrs.at[0], up),
        remote(lat_h.at[pl.ds(0, W)], halo.at[1], hss.at[1], hrs.at[1], down),
    ]
    for c in halos:
        c.start()

    def block(s, low=0, rows=T):
        return kv.at[pl.ds(s * T + low, rows)]

    def passed(i, src, dst, low, rows, dev):
        return remote(block(src, low, rows), block(dst, low, rows), kss.at[i], krs.at[i], dev)

    wave1 = [
        remote(stale_h, block(1), kss.at[0], krs.at[0], y_up),
        remote(stale_h, block(2), kss.at[1], krs.at[1], y_down),
        remote(stale_h, block(3), kss.at[2], krs.at[2], x_other),
    ]
    wave2 = [
        passed(3, 1, 6, 128, 64, x_other),
        passed(5, 3, 6, 0, 128, y_up),
        passed(6, 3, 7, 256, 128, y_down),
        passed(4, 2, 7, 192, 64, x_other),
        passed(7, 1, 5, 0, 192, y_up),
        passed(8, 2, 5, 192, 192, y_down),
        passed(9, 1, 6, 192, 192, x_other),
        passed(10, 2, 7, 0, 192, x_other),
    ]
    wave3 = [
        passed(11, 6, 8, 0, 192, y_up),
        passed(12, 7, 8, 192, 192, y_down),
    ]
    for c in wave1:
        c.start()

    for c in st1:
        c.wait_recv()
    stat2[0] = jnp.sum(stat1[...], axis=0)
    st2 = [remote(stat2.at[0], stat2.at[s], s2s.at[s - 1], s2r.at[s - 1], z_peers[s]) for s in (1, 3, 2)]
    for c in st2:
        c.start()
    loads[1].wait()
    for c in st2:
        c.wait_recv()
    total = jnp.sum(stat2[...], axis=0)
    total8 = jnp.where(row8 == 0, total[0:1], jnp.where(row8 == 1, total[1:2], 0.0))
    hi = total8.astype(BF).astype(F32)
    mid = (total8 - hi).astype(BF).astype(F32)
    low = total8 - hi - mid
    parts = jnp.concatenate([hi, mid, low, jnp.zeros((8, C), F32)], axis=0).astype(BF)
    summed = jnp.dot(parts, gmat[...], preferred_element_type=F32)
    summed = summed[0:8] + summed[8:16] + summed[16:24]
    count = float(32 * T * (C // GROUPS))
    center = summed[0:1] / count
    variance = summed[1:2] / count - center * center
    scale = lax.rsqrt(variance + 1e-05)
    gain = gain_ref[...].reshape(1, C)
    bias = bias_ref[...].reshape(1, C)

    wrow = lax.broadcasted_iota(jnp.int32, (W, C), 0)

    def hidden_row(block, r, keep):
        v = (block.astype(F32) - center) * scale * gain + bias
        h = v / (1.0 + jnp.exp(-v))
        if keep is not None:
            h = jnp.where(keep, h, 0.0)
        rows = pl.ds(r * W, W)
        hcat[rows, 0:C] = jnp.where(wrow == 0, 0.0, pltpu.roll(h, 1, 0)).astype(BF)
        hcat[rows, C : 2 * C] = h.astype(BF)
        hcat[rows, 2 * C : 3 * C] = jnp.where(wrow == W - 1, 0.0, pltpu.roll(h, W - 1, 0)).astype(BF)

    hidden_row(lat[0:W], 1, None)
    hidden_row(lat[W : 2 * W], 2, None)
    loads[2].wait()
    cacc[...] = jnp.dot(hcat[W : W + T], convw[1], preferred_element_type=F32)
    halos[0].wait_recv()
    halos[1].wait_recv()
    hidden_row(halo[0], 0, p > 0)
    hidden_row(halo[1], 3, p < 31)
    cacc[...] += jnp.dot(hcat[0:T], convw[0], preferred_element_type=F32)
    cacc[...] += jnp.dot(hcat[2 * W : 2 * W + T], convw[2], preferred_element_type=F32)
    resid[...] = (lat[...].astype(F32) + cacc[...]).astype(BF)

    def half(h):
        return pl.ds(pl.multiple_of(h * HALF, HALF), HALF)

    def q_copy(s, h, dev, src=0):
        i = (s - 1) * 2 + h
        return remote(qbuf.at[src, half(h)], qbuf.at[s, half(h)], qss.at[i], qrs.at[i], dev)

    loads[3].wait()
    loads[4].wait()
    qbuf[0] = (jnp.dot(resid[...], wqkv[:, 0:HC], preferred_element_type=F32) * SCALE).astype(BF)
    q_sends = [q_copy(s, h, z_peers[s]) for h in (0, 1) for s in (1, 3)]
    for c in q_sends:
        c.start()
    kv[0:T] = jnp.dot(resid[...], wqkv[:, HC:], preferred_element_type=F32).astype(BF)
    fresh_copy = pltpu.make_async_copy(kv.at[pl.ds(0, T)], fresh_h, lsem.at[10])
    fresh_copy.start()

    for c in wave1:
        c.wait_recv()
    for c in wave2:
        c.start()
    loads[5].wait()

    lane = lax.broadcasted_iota(jnp.int32, (HALF, 128), 1)
    first = lane < HEAD
    ones = jnp.ones((CHUNK, 128), BF)

    def scores(qs, rows, row0, h):
        q = qbuf[qs, rows, (h // 2) * 128 : (h // 2) * 128 + 128]
        q = jnp.where(first if h % 2 == 0 else ~first, q, jnp.zeros_like(q))
        k = kv[pl.ds(row0, CHUNK), (h // 2) * 128 : (h // 2) * 128 + 128]
        return lax.dot_general(q, k, (((1,), (1,)), ((), ())), preferred_element_type=F32)

    def weigh(row0, h, prob):
        v = kv[pl.ds(row0, CHUNK), HC + (h // 2) * 128 : HC + (h // 2) * 128 + 128]
        return jnp.dot(prob, jnp.concatenate([v, ones], axis=1), preferred_element_type=F32)

    def pipeline(soft, done, qs, rows, row0):
        ss, ps = {}, {}
        for i in range(HEADS + 2):
            if i < HEADS:
                ss[i] = scores(qs, rows, row0, i)
            if 0 <= i - 1 < HEADS:
                ps[i - 1] = soft(ss.pop(i - 1), i - 1)
            if 0 <= i - 2 < HEADS:
                prob, extra = ps.pop(i - 2)
                done(i - 2, weigh(row0, i - 2, prob), extra)

    def first_chunk(t, carry):
        qs = jnp.where(t < 2, 0, jnp.where(t < 6, 1 + 2 * (t % 2), 2))
        hh = jnp.where(t < 2, t, jnp.where(t < 6, (t - 2) // 2, t - 6))
        rows = half(hh)
        row0 = pl.multiple_of(jnp.where(t < 2, 0, T), T)

        @pl.when(t >= 2)
        def _():
            q_copy(qs, hh, z_peers[1]).wait_recv()

        @pl.when((t == 2) | (t == 4))
        def _():
            q_copy(2, hh, z_peers[1], src=1).start()

        @pl.when(t == 4)
        def _():
            for c in wave2[:4]:
                c.wait_recv()
            for c in wave3:
                c.start()

        def soft(s, h):
            top = jnp.max(s, axis=1, keepdims=True)
            mbuf[qs, h, rows] = jnp.broadcast_to(top, (HALF, 128))
            return jnp.exp2(s - top).astype(BF), None

        held = {}

        def done(h, r, _):
            lbuf[qs, h, rows] = r[:, 128:]
            if h % 2 == 0:
                held[0] = r[:, :128]
            else:
                acc[qs, h // 2, rows] = jnp.where(first, held.pop(0), r[:, :128])

        pipeline(soft, done, qs, rows, row0)
        return carry

    lax.fori_loop(0, 8, first_chunk, 0)

    for c in wave2[4:] + wave3:
        c.wait_recv()

    def part_copies(s, h, dev):
        i = s * 2 + h
        return [
            remote(pout.at[s, half(h)], pin.at[s, half(h)], pss.at[i], prs.at[i], dev),
            remote(lout.at[s, h], lin.at[s, h], lss.at[i], lrs.at[i], dev),
        ]

    def quarter(h, g):
        return pl.ds(pl.multiple_of(h * HALF + g * QTR, QTR), QTR)

    def unit_copy(d, h):
        i = (d - 1) * 2 + h
        return remote(units.at[quarter(h, f_ids[d])], ubuf.at[quarter(h, d)], uss.at[i], urs.at[i], f_peers[d])

    def back_copy(d, h, owner):
        i = (d - 1) * 2 + h
        return remote(tres.at[h, d], tbuf.at[quarter(h, owner)], tss.at[i], trs.at[i], f_peers[d])

    def combine(h):
        rows = half(h)
        for s in (3, 2, 1):
            for c in part_copies(s, h, z_back[s]):
                c.wait_recv()
        lse = [lout[0, h], lin[1, h], lin[2, h], lin[3, h]]
        top = jnp.maximum(jnp.maximum(lse[0], lse[1]), jnp.maximum(lse[2], lse[3]))
        ws = [jnp.exp2(v - top) for v in lse]
        tot = ws[0] + ws[1] + ws[2] + ws[3]
        ws = [jnp.transpose(v / tot)[0:HALF] for v in ws]
        pairs = []
        for hp in range(HEADS // 2):
            cols = slice(hp * 128, hp * 128 + 128)
            o = None
            for s in range(4):
                part = (pout[0, rows, cols] if s == 0 else pin[s, rows, cols]).astype(F32)
                wgt = jnp.where(first, ws[s][:, 2 * hp : 2 * hp + 1], ws[s][:, 2 * hp + 1 : 2 * hp + 2])
                o = part * wgt if o is None else o + part * wgt
            pairs.append(o.astype(BF))
        attn = jnp.concatenate(pairs, axis=1)
        mixed = (resid[rows].astype(F32) + jnp.dot(attn, wout[...], preferred_element_type=F32)).astype(BF)
        resid[rows] = mixed
        mixed = mixed.astype(F32)
        mean = jnp.mean(mixed, axis=1, keepdims=True)
        dev = mixed - mean
        var = jnp.mean(dev * dev, axis=1, keepdims=True)
        lgain = lgain_ref[...].reshape(1, C)
        lbias = lbias_ref[...].reshape(1, C)
        units[rows] = (dev * lax.rsqrt(var + 1e-05) * lgain + lbias + code_ref[pl.ds(f, 1), :]).astype(BF)
        for d in (2, 3, 1):
            unit_copy(d, h).start()
        ubuf[quarter(h, 0)] = units[quarter(h, f)]

    def temporal(h):
        for d in (1, 2, 3):
            unit_copy(d, h).wait_recv()
        tqkv = jnp.dot(ubuf[half(h)], wt[...], preferred_element_type=F32).astype(BF).astype(F32)
        for a in (2, 3, 1, 0):
            tq = tqkv[a * QTR : (a + 1) * QTR, 0:C]
            his, los = [], []
            for b in range(FRAMES):
                prod = tq * tqkv[b * QTR : (b + 1) * QTR, C : 2 * C]
                phi = prod.astype(BF)
                his.append(phi)
                los.append((prod - phi.astype(F32)).astype(BF))
            lhs = jnp.concatenate([jnp.concatenate(his, axis=0), jnp.concatenate(los, axis=0)], axis=1)
            sc = jnp.dot(lhs, hsum_ref[...], preferred_element_type=F32) * THEAD ** (-0.5)
            sc = [sc[b * QTR : (b + 1) * QTR] for b in range(FRAMES)]
            top = jnp.maximum(jnp.maximum(sc[0], sc[1]), jnp.maximum(sc[2], sc[3]))
            es = [jnp.exp(v - top) for v in sc]
            rec = 1.0 / (es[0] + es[1] + es[2] + es[3])
            rhi = rec.astype(BF)
            rlo = (rec - rhi.astype(F32)).astype(BF)
            wide_rows = jnp.concatenate([e.astype(BF) for e in es] + [rhi, rlo], axis=0)
            ex = jnp.dot(wide_rows, hexp_ref[...], preferred_element_type=F32)
            o = None
            for b in range(FRAMES):
                term = ex[b * QTR : (b + 1) * QTR] * tqkv[b * QTR : (b + 1) * QTR, 2 * C : 3 * C]
                o = term if o is None else o + term
            o = (o * (ex[4 * QTR : 5 * QTR] + ex[5 * QTR : 6 * QTR])).astype(BF)
            if a == 0:
                tbuf[quarter(h, f)] = o
            else:
                tres[h, a] = o
                back_copy(a, h, f).start()

    def finish(h):
        for d in (1, 2, 3):
            back_copy(d, h, f_ids[d]).wait_recv()
        rows = half(h)
        out_ref[rows] = resid[rows].astype(F32) + jnp.dot(tbuf[rows], tout[...], preferred_element_type=F32)

    for i in (6, 7, 8, 9, 10, 11):
        loads[i].wait()

    def second_chunk(t, carry):
        qs = jnp.where(t < 6, 3 - t % 3, 0)
        hh = jnp.where(t < 6, t // 3, t - 6)
        rows = half(hh)
        row0 = 5 * T

        def soft(s, h):
            old = mbuf[qs, h, rows]
            new = jnp.maximum(old, jnp.max(s, axis=1, keepdims=True))
            return jnp.exp2(s - new[:, :1]).astype(BF), (new, jnp.exp2(old - new))

        held = {}
        lses = jnp.zeros((HALF, 128), F32)

        def done(h, r, extra):
            nonlocal lses
            new, shrink = extra
            tot = lbuf[qs, h, rows] * shrink + r[:, 128:]
            lses = jnp.where(lane == h, new + jnp.log2(tot), lses)
            o = acc[qs, h // 2, rows] * shrink + r[:, :128]
            o = o / tot
            if h % 2 == 0:
                held[0] = o
            else:
                pout[qs, rows, (h // 2) * 128 : (h // 2) * 128 + 128] = jnp.where(first, held.pop(0), o).astype(BF)

        pipeline(soft, done, qs, rows, row0)
        lses = jnp.concatenate([lses, jnp.zeros((LSE - HALF, 128), F32)], axis=0)
        lout[qs, hh] = jnp.transpose(lses)[0:8]

        @pl.when(qs > 0)
        def _():
            for c in part_copies(qs, hh, at(x, y, (z + 4 - qs) % 4)):
                c.start()

        @pl.when(t == 6)
        def _():
            combine(0)

        return carry

    lax.fori_loop(0, 8, second_chunk, 0)
    combine(1)
    temporal(0)
    temporal(1)
    finish(0)
    finish(1)

    fresh_copy.wait()
    for c in st1 + halos + wave1 + wave2 + wave3 + st2 + q_sends:
        c.wait_send()
    for h in (0, 1):
        q_copy(2, h, z_peers[1], src=1).wait_send()
        for s in (1, 2, 3):
            for c in part_copies(s, h, z_back[s]):
                c.wait_send()
            unit_copy(s, h).wait_send()
            back_copy(s, h, f).wait_send()


def deliver(out_in, fresh_in, out, fresh, held_out, held_fresh, sems):
    steps = []
    for i in range(PARTS):
        rows = pl.ds(i * (T // PARTS), T // PARTS)
        for k, (src, held, dst) in enumerate(((out_in, held_out, out), (fresh_in, held_fresh, fresh))):
            steps.append(
                (
                    pltpu.make_async_copy(src.at[rows], held.at[rows], sems.at[k, i]),
                    pltpu.make_async_copy(held.at[rows], dst.at[rows], sems.at[2 + k, i]),
                )
            )
    for load, _ in steps:
        load.start()
    for load, store in steps:
        load.wait()
        store.start()
    for _, store in steps:
        store.wait()


def codes():
    halves = np.arange(C // 2, dtype=np.float64)
    freqs = np.exp(-math.log(10000.0) * 2.0 * halves / C)
    angles = np.arange(FRAMES)[:, None] * freqs[None, :]
    table = np.stack([np.sin(angles), np.cos(angles)], axis=-1).reshape(FRAMES, C)
    return np.concatenate([table, np.zeros((8 - FRAMES, C))]).astype(np.float32)


def shards(
    latent, gn_gain, gn_bias, conv_weight, w_query, w_kv, w_out, stale_kv, ln_gain, ln_bias, t_query, t_kv, t_out
):
    group = np.arange(C) // (C // GROUPS)
    gmat = jnp.asarray((group[:, None] == group[None, :]).astype(np.float32), BF)
    head = (np.arange(C)[:, None] // THEAD == np.arange(128)[None, :]).astype(np.float32)
    hsum = jnp.asarray(np.concatenate([head, head]), BF)
    hexp = jnp.asarray(head.T.copy(), BF)
    hbm = pl.BlockSpec(memory_space=pl.ANY)
    vmem = pl.BlockSpec(memory_space=pltpu.VMEM)
    dma = pltpu.SemaphoreType.DMA
    out, fresh = pl.pallas_call(
        kernel,
        out_shape=(jax.ShapeDtypeStruct((T, C), F32), jax.ShapeDtypeStruct((T, 2 * HC), BF)),
        in_specs=[hbm] * 9 + [vmem] * 5 + [hbm] * 3,
        out_specs=(vmem, hbm),
        scratch_shapes=[
            pltpu.VMEM((T, C), BF),
            pltpu.VMEM((2, W, C), BF),
            pltpu.VMEM((3, 3 * C, C), BF),
            pltpu.VMEM((C, 3 * HC), BF),
            pltpu.VMEM((HC, C), BF),
            pltpu.VMEM((C, 3 * C), BF),
            pltpu.VMEM((C, C), BF),
            pltpu.VMEM((C, C), BF),
            pltpu.VMEM((4 * W, 3 * C), BF),
            pltpu.VMEM((T, C), F32),
            pltpu.VMEM((T, C), BF),
            pltpu.VMEM((8, 2, C), F32),
            pltpu.VMEM((4, 2, C), F32),
            pltpu.VMEM((4, T, HC), BF),
            pltpu.VMEM((9 * T, 2 * HC), BF),
            pltpu.VMEM((4, HEADS // 2, T, 128), F32),
            pltpu.VMEM((4, HEADS, T, 128), F32),
            pltpu.VMEM((4, HEADS, T, 128), F32),
            pltpu.VMEM((4, T, HC), BF),
            pltpu.VMEM((4, T, HC), BF),
            pltpu.VMEM((4, 2, 8, LSE), F32),
            pltpu.VMEM((4, 2, 8, LSE), F32),
            pltpu.VMEM((T, C), BF),
            pltpu.VMEM((T, C), BF),
            pltpu.VMEM((2, 4, QTR, C), BF),
            pltpu.VMEM((T, C), BF),
            pltpu.VMEM((2 * C, 128), BF),
            pltpu.VMEM((128, C), BF),
            dma((13,)), dma((2,)), dma((2,)), dma((7,)), dma((7,)), dma((3,)), dma((3,)),
            dma((13,)), dma((13,)), dma((6,)), dma((6,)), dma((8,)), dma((8,)), dma((8,)), dma((8,)),
            dma((6,)), dma((6,)), dma((6,)), dma((6,)),
        ],
        compiler_params=pltpu.CompilerParams(
            collective_id=0, has_side_effects=True, vmem_limit_bytes=63 * 2**20
        ),
    )(
        latent.reshape(T, C),
        stale_kv.reshape(T, 2 * HC),
        conv_weight.reshape(3, 3 * C, C),
        w_query,
        w_kv,
        w_out,
        t_query,
        t_kv,
        t_out,
        gn_gain,
        gn_bias,
        ln_gain,
        ln_bias,
        jnp.asarray(codes()),
        gmat,
        hsum,
        hexp,
    )
    out, fresh = pl.pallas_call(
        deliver,
        out_shape=(jax.ShapeDtypeStruct((T, C), F32), jax.ShapeDtypeStruct((T, 2 * HC), BF)),
        in_specs=[hbm] * 2,
        out_specs=(hbm, hbm),
        scratch_shapes=[pltpu.VMEM((T, C), F32), pltpu.VMEM((T, 2 * HC), BF), dma((4, PARTS))],
    )(out, fresh)
    return out.reshape(1, 2, W, C), fresh.reshape(1, 2, W, 2 * HC)


def solution(mesh):
    sharded = P("frame", "patch", None, None)
    placed = (sharded,) + (P(),) * 6 + (sharded,) + (P(),) * 5
    return jax.shard_map(
        shards, mesh=mesh, in_specs=placed, out_specs=(sharded, sharded), check_vma=False
    )
```

```python
import math

import jax
import jax.numpy as jnp
import numpy as np
from jax import lax
from jax.experimental import pallas as pl
from jax.experimental.pallas import tpu as pltpu
from jax.sharding import PartitionSpec as P

C = 640
THEADS = 8
GROUPS = 32
HEADS = 6
HEAD = 64
THEAD = 80
HC = 384
W = 192
T = 384
FRAMES = 4
HALF = 192
QTR = 48
LSE = 256
PARTS = 4
CHUNK = 1536
BF = jnp.bfloat16
F32 = jnp.float32
SCALE = HEAD ** (-0.5) * math.log2(math.e)
MESH = pl.DeviceIdType.MESH


def kernel(
    lat_h, stale_h, convw_h, wq_h, wkv_h, wout_h, tq_h, tkv_h, tout_h,
    gain_ref, bias_ref, lgain_ref, lbias_ref, code_ref, gmat_h, hsum_h, hexp_h,
    out_ref, fresh_h,
    lat, halo, convw, wqkv, wout, wt, tout, gmat, hcat, cacc, resid,
    stat1, stat2, qbuf, kv, acc, lbuf, mbuf, pout, pin, lout, lin,
    units, ubuf, tres, tbuf, hsum_ref, hexp_ref,
    lsem, hss, hrs, s1s, s1r, s2s, s2r, kss, krs, qss, qrs, pss, prs, lss, lrs, uss, urs, tss, trs,
):
    f = lax.axis_index("frame")
    p = lax.axis_index("patch")
    x = p // 16
    y = (p // 4) % 4
    z = p % 4

    def at(px, py, pz):
        return (f, px * 16 + py * 4 + pz)

    def remote(src, dst, ss, rs, dev):
        return pltpu.make_async_remote_copy(
            src_ref=src, dst_ref=dst, send_sem=ss, recv_sem=rs, device_id=dev, device_id_type=MESH
        )

    xy = [((x + dx) % 2, (y + dy) % 4) for dx, dy in ((0, 1), (0, 3), (1, 0), (0, 2), (1, 1), (1, 3), (1, 2))]
    xy_peers = [at(a, b, z) for a, b in xy]
    y_up, y_down, x_other = xy_peers[:3]
    z_peers = {s: at(x, y, (z + s) % 4) for s in (1, 2, 3)}
    z_back = {s: at(x, y, (z + 4 - s) % 4) for s in (1, 2, 3)}
    up = (f, (p + 1) % 32)
    down = (f, (p + 31) % 32)
    f_ids = {0: f, 1: f + 1 - 2 * (f % 2), 2: (f + 2) % 4, 3: 3 - f}
    f_peers = {d: (f_ids[d], p) for d in (1, 2, 3)}

    loads = [
        pltpu.make_async_copy(lat_h, lat, lsem.at[0]),
        pltpu.make_async_copy(gmat_h, gmat, lsem.at[1]),
        pltpu.make_async_copy(convw_h, convw, lsem.at[2]),
        pltpu.make_async_copy(wq_h, wqkv.at[:, pl.ds(0, HC)], lsem.at[3]),
        pltpu.make_async_copy(wkv_h, wqkv.at[:, pl.ds(HC, 2 * HC)], lsem.at[4]),
        pltpu.make_async_copy(stale_h, kv.at[pl.ds(4 * T, T)], lsem.at[5]),
        pltpu.make_async_copy(wout_h, wout, lsem.at[6]),
        pltpu.make_async_copy(tq_h, wt.at[:, pl.ds(0, C)], lsem.at[7]),
        pltpu.make_async_copy(tkv_h, wt.at[:, pl.ds(C, 2 * C)], lsem.at[8]),
        pltpu.make_async_copy(tout_h, tout, lsem.at[9]),
        pltpu.make_async_copy(hsum_h, hsum_ref, lsem.at[11]),
        pltpu.make_async_copy(hexp_h, hexp_ref, lsem.at[12]),
    ]
    loads[0].start()

    barrier = pltpu.get_barrier_semaphore()
    greet = xy_peers + list(z_peers.values()) + [up, down] + list(f_peers.values())
    for dev in greet:
        pl.semaphore_signal(barrier, inc=1, device_id=dev, device_id_type=MESH)

    row8 = lax.broadcasted_iota(jnp.int32, (8, C), 0)
    loads[0].wait()
    wide = lat[...].astype(F32)
    stat1[0, 0:1, :] = jnp.sum(wide, axis=0, keepdims=True)
    stat1[0, 1:2, :] = jnp.sum(wide * wide, axis=0, keepdims=True)
    pl.semaphore_wait(barrier, len(greet))

    st1 = [remote(stat1.at[0], stat1.at[1 + i], s1s.at[i], s1r.at[i], d) for i, d in enumerate(xy_peers)]
    for c in st1:
        c.start()
    halos = [
        remote(lat_h.at[pl.ds(W, W)], halo.at[0], hss.at[0], hrs.at[0], up),
        remote(lat_h.at[pl.ds(0, W)], halo.at[1], hss.at[1], hrs.at[1], down),
    ]
    for c in halos:
        c.start()

    def block(s, low=0, rows=T):
        return kv.at[pl.ds(s * T + low, rows)]

    def passed(i, src, dst, low, rows, dev):
        return remote(block(src, low, rows), block(dst, low, rows), kss.at[i], krs.at[i], dev)

    wave1 = [
        remote(stale_h, block(1), kss.at[0], krs.at[0], y_up),
        remote(stale_h, block(2), kss.at[1], krs.at[1], y_down),
        remote(stale_h, block(3), kss.at[2], krs.at[2], x_other),
    ]
    wave2 = [
        passed(3, 1, 6, 128, 64, x_other),
        passed(5, 3, 6, 0, 128, y_up),
        passed(6, 3, 7, 256, 128, y_down),
        passed(4, 2, 7, 192, 64, x_other),
        passed(7, 1, 5, 0, 192, y_up),
        passed(8, 2, 5, 192, 192, y_down),
        passed(9, 1, 6, 192, 192, x_other),
        passed(10, 2, 7, 0, 192, x_other),
    ]
    wave3 = [
        passed(11, 6, 8, 0, 192, y_up),
        passed(12, 7, 8, 192, 192, y_down),
    ]
    for c in wave1:
        c.start()
    for c in loads[1:]:
        c.start()

    for c in st1:
        c.wait_recv()
    stat2[0] = jnp.sum(stat1[...], axis=0)
    st2 = [remote(stat2.at[0], stat2.at[s], s2s.at[s - 1], s2r.at[s - 1], z_peers[s]) for s in (1, 3, 2)]
    for c in st2:
        c.start()
    loads[1].wait()
    for c in st2:
        c.wait_recv()
    total = jnp.sum(stat2[...], axis=0)
    total8 = jnp.where(row8 == 0, total[0:1], jnp.where(row8 == 1, total[1:2], 0.0))
    hi = total8.astype(BF).astype(F32)
    mid = (total8 - hi).astype(BF).astype(F32)
    low = total8 - hi - mid
    parts = jnp.concatenate([hi, mid, low, jnp.zeros((8, C), F32)], axis=0).astype(BF)
    summed = jnp.dot(parts, gmat[...], preferred_element_type=F32)
    summed = summed[0:8] + summed[8:16] + summed[16:24]
    count = float(32 * T * (C // GROUPS))
    center = summed[0:1] / count
    variance = summed[1:2] / count - center * center
    scale = lax.rsqrt(variance + 1e-05)
    gain = gain_ref[...].reshape(1, C)
    bias = bias_ref[...].reshape(1, C)

    wrow = lax.broadcasted_iota(jnp.int32, (W, C), 0)

    def hidden_row(block, r, keep):
        v = (block.astype(F32) - center) * scale * gain + bias
        h = v / (1.0 + jnp.exp(-v))
        if keep is not None:
            h = jnp.where(keep, h, 0.0)
        rows = pl.ds(r * W, W)
        hcat[rows, 0:C] = jnp.where(wrow == 0, 0.0, pltpu.roll(h, 1, 0)).astype(BF)
        hcat[rows, C : 2 * C] = h.astype(BF)
        hcat[rows, 2 * C : 3 * C] = jnp.where(wrow == W - 1, 0.0, pltpu.roll(h, W - 1, 0)).astype(BF)

    hidden_row(lat[0:W], 1, None)
    hidden_row(lat[W : 2 * W], 2, None)
    loads[2].wait()
    cacc[...] = jnp.dot(hcat[W : W + T], convw[1], preferred_element_type=F32)
    cacc[0:W] += jnp.dot(hcat[2 * W : 3 * W], convw[2], preferred_element_type=F32)
    cacc[W:T] += jnp.dot(hcat[W : 2 * W], convw[0], preferred_element_type=F32)
    halos[0].wait_recv()
    halos[1].wait_recv()
    hidden_row(halo[0], 0, p > 0)
    hidden_row(halo[1], 3, p < 31)
    cacc[0:W] += jnp.dot(hcat[0:W], convw[0], preferred_element_type=F32)
    cacc[W:T] += jnp.dot(hcat[3 * W : 4 * W], convw[2], preferred_element_type=F32)
    resid[...] = (lat[...].astype(F32) + cacc[...]).astype(BF)

    def half(h):
        return pl.ds(pl.multiple_of(h * HALF, HALF), HALF)

    def q_copy(s, h, dev, src=0):
        i = (s - 1) * 2 + h
        return remote(qbuf.at[src, half(h)], qbuf.at[s, half(h)], qss.at[i], qrs.at[i], dev)

    loads[3].wait()
    loads[4].wait()
    qbuf[0] = (jnp.dot(resid[...], wqkv[:, 0:HC], preferred_element_type=F32) * SCALE).astype(BF)
    q_sends = [q_copy(s, h, z_peers[s]) for h in (0, 1) for s in (1, 3)]
    for c in q_sends:
        c.start()
    kv[0:T] = jnp.dot(resid[...], wqkv[:, HC:], preferred_element_type=F32).astype(BF)
    fresh_copy = pltpu.make_async_copy(kv.at[pl.ds(0, T)], fresh_h, lsem.at[10])
    fresh_copy.start()

    for c in wave1:
        c.wait_recv()
    for c in wave2:
        c.start()
    loads[5].wait()

    lane = lax.broadcasted_iota(jnp.int32, (HALF, 128), 1)
    first = lane < HEAD
    ones = jnp.ones((CHUNK, 128), BF)

    def scores(qs, rows, row0, h):
        q = qbuf[qs, rows, (h // 2) * 128 : (h // 2) * 128 + 128]
        q = jnp.where(first if h % 2 == 0 else ~first, q, jnp.zeros_like(q))
        k = kv[pl.ds(row0, CHUNK), (h // 2) * 128 : (h // 2) * 128 + 128]
        return lax.dot_general(q, k, (((1,), (1,)), ((), ())), preferred_element_type=F32)

    def weigh(row0, h, prob):
        v = kv[pl.ds(row0, CHUNK), HC + (h // 2) * 128 : HC + (h // 2) * 128 + 128]
        return jnp.dot(prob, jnp.concatenate([v, ones], axis=1), preferred_element_type=F32)

    def pipeline(soft, done, qs, rows, row0):
        ss, ps = {}, {}
        for i in range(HEADS + 2):
            if i < HEADS:
                ss[i] = scores(qs, rows, row0, i)
            if 0 <= i - 1 < HEADS:
                ps[i - 1] = soft(ss.pop(i - 1), i - 1)
            if 0 <= i - 2 < HEADS:
                prob, extra = ps.pop(i - 2)
                done(i - 2, weigh(row0, i - 2, prob), extra)

    def first_chunk(t, carry):
        qs = jnp.where(t < 2, 0, jnp.where(t < 6, 1 + 2 * (t % 2), 2))
        hh = jnp.where(t < 2, t, jnp.where(t < 6, (t - 2) // 2, t - 6))
        rows = half(hh)
        row0 = pl.multiple_of(jnp.where(t < 2, 0, T), T)

        @pl.when(t >= 2)
        def _():
            q_copy(qs, hh, z_peers[1]).wait_recv()

        @pl.when((t == 2) | (t == 4))
        def _():
            q_copy(2, hh, z_peers[1], src=1).start()

        @pl.when(t == 4)
        def _():
            for c in wave2[:4]:
                c.wait_recv()
            for c in wave3:
                c.start()

        def soft(s, h):
            top = jnp.max(s, axis=1, keepdims=True)
            mbuf[qs, h, rows] = jnp.broadcast_to(top, (HALF, 128))
            return jnp.exp2(s - top).astype(BF), None

        held = {}

        def done(h, r, _):
            lbuf[qs, h, rows] = r[:, 128:]
            if h % 2 == 0:
                held[0] = r[:, :128]
            else:
                acc[qs, h // 2, rows] = jnp.where(first, held.pop(0), r[:, :128])

        pipeline(soft, done, qs, rows, row0)
        return carry

    lax.fori_loop(0, 8, first_chunk, 0)

    for c in wave2[4:] + wave3:
        c.wait_recv()

    def part_copies(s, h, dev):
        i = s * 2 + h
        return [
            remote(pout.at[s, half(h)], pin.at[s, half(h)], pss.at[i], prs.at[i], dev),
            remote(lout.at[s, h], lin.at[s, h], lss.at[i], lrs.at[i], dev),
        ]

    def quarter(h, g):
        return pl.ds(pl.multiple_of(h * HALF + g * QTR, QTR), QTR)

    def unit_copy(d, h):
        i = (d - 1) * 2 + h
        return remote(units.at[quarter(h, f_ids[d])], ubuf.at[quarter(h, d)], uss.at[i], urs.at[i], f_peers[d])

    def back_copy(d, h, owner):
        i = (d - 1) * 2 + h
        return remote(tres.at[h, d], tbuf.at[quarter(h, owner)], tss.at[i], trs.at[i], f_peers[d])

    def combine(h):
        rows = half(h)
        for s in (3, 2, 1):
            for c in part_copies(s, h, z_back[s]):
                c.wait_recv()
        lse = [lout[0, h], lin[1, h], lin[2, h], lin[3, h]]
        top = jnp.maximum(jnp.maximum(lse[0], lse[1]), jnp.maximum(lse[2], lse[3]))
        ws = [jnp.exp2(v - top) for v in lse]
        tot = ws[0] + ws[1] + ws[2] + ws[3]
        ws = [jnp.transpose(v / tot)[0:HALF] for v in ws]
        pairs = []
        for hp in range(HEADS // 2):
            cols = slice(hp * 128, hp * 128 + 128)
            o = None
            for s in range(4):
                part = (pout[0, rows, cols] if s == 0 else pin[s, rows, cols]).astype(F32)
                wgt = jnp.where(first, ws[s][:, 2 * hp : 2 * hp + 1], ws[s][:, 2 * hp + 1 : 2 * hp + 2])
                o = part * wgt if o is None else o + part * wgt
            pairs.append(o.astype(BF))
        attn = jnp.concatenate(pairs, axis=1)
        mixed = (resid[rows].astype(F32) + jnp.dot(attn, wout[...], preferred_element_type=F32)).astype(BF)
        resid[rows] = mixed
        mixed = mixed.astype(F32)
        mean = jnp.mean(mixed, axis=1, keepdims=True)
        dev = mixed - mean
        var = jnp.mean(dev * dev, axis=1, keepdims=True)
        lgain = lgain_ref[...].reshape(1, C)
        lbias = lbias_ref[...].reshape(1, C)
        units[rows] = (dev * lax.rsqrt(var + 1e-05) * lgain + lbias + code_ref[pl.ds(f, 1), :]).astype(BF)
        for d in (2, 3, 1):
            unit_copy(d, h).start()
        ubuf[quarter(h, 0)] = units[quarter(h, f)]

    def temporal(h):
        for d in (1, 2, 3):
            unit_copy(d, h).wait_recv()
        tqkv = jnp.dot(ubuf[half(h)], wt[...], preferred_element_type=F32).astype(BF).astype(F32)
        for a in (2, 3, 1, 0):
            tq = tqkv[a * QTR : (a + 1) * QTR, 0:C]
            his, los = [], []
            for b in range(FRAMES):
                prod = tq * tqkv[b * QTR : (b + 1) * QTR, C : 2 * C]
                phi = prod.astype(BF)
                his.append(phi)
                los.append((prod - phi.astype(F32)).astype(BF))
            lhs = jnp.concatenate([jnp.concatenate(his, axis=0), jnp.concatenate(los, axis=0)], axis=1)
            sc = jnp.dot(lhs, hsum_ref[...], preferred_element_type=F32) * THEAD ** (-0.5)
            sc = [sc[b * QTR : (b + 1) * QTR] for b in range(FRAMES)]
            top = jnp.maximum(jnp.maximum(sc[0], sc[1]), jnp.maximum(sc[2], sc[3]))
            es = [jnp.exp(v - top) for v in sc]
            rec = 1.0 / (es[0] + es[1] + es[2] + es[3])
            rhi = rec.astype(BF)
            rlo = (rec - rhi.astype(F32)).astype(BF)
            wide_rows = jnp.concatenate([e.astype(BF) for e in es] + [rhi, rlo], axis=0)
            ex = jnp.dot(wide_rows, hexp_ref[...], preferred_element_type=F32)
            o = None
            for b in range(FRAMES):
                term = ex[b * QTR : (b + 1) * QTR] * tqkv[b * QTR : (b + 1) * QTR, 2 * C : 3 * C]
                o = term if o is None else o + term
            o = (o * (ex[4 * QTR : 5 * QTR] + ex[5 * QTR : 6 * QTR])).astype(BF)
            if a == 0:
                tbuf[quarter(h, f)] = o
            else:
                tres[h, a] = o
                back_copy(a, h, f).start()

    def finish(h):
        for d in (1, 2, 3):
            back_copy(d, h, f_ids[d]).wait_recv()
        rows = half(h)
        out_ref[rows] = resid[rows].astype(F32) + jnp.dot(tbuf[rows], tout[...], preferred_element_type=F32)

    for i in (6, 7, 8, 9, 10, 11):
        loads[i].wait()

    def second_chunk(t, carry):
        qs = jnp.where(t < 6, 3 - t % 3, 0)
        hh = jnp.where(t < 6, t // 3, t - 6)
        rows = half(hh)
        row0 = 5 * T

        def soft(s, h):
            old = mbuf[qs, h, rows]
            new = jnp.maximum(old, jnp.max(s, axis=1, keepdims=True))
            return jnp.exp2(s - new[:, :1]).astype(BF), (new, jnp.exp2(old - new))

        held = {}
        lses = jnp.zeros((HALF, 128), F32)

        def done(h, r, extra):
            nonlocal lses
            new, shrink = extra
            tot = lbuf[qs, h, rows] * shrink + r[:, 128:]
            lses = jnp.where(lane == h, new + jnp.log2(tot), lses)
            o = acc[qs, h // 2, rows] * shrink + r[:, :128]
            o = o / tot
            if h % 2 == 0:
                held[0] = o
            else:
                pout[qs, rows, (h // 2) * 128 : (h // 2) * 128 + 128] = jnp.where(first, held.pop(0), o).astype(BF)

        pipeline(soft, done, qs, rows, row0)
        lses = jnp.concatenate([lses, jnp.zeros((LSE - HALF, 128), F32)], axis=0)
        lout[qs, hh] = jnp.transpose(lses)[0:8]

        @pl.when(qs > 0)
        def _():
            for c in part_copies(qs, hh, at(x, y, (z + 4 - qs) % 4)):
                c.start()

        @pl.when(t == 6)
        def _():
            combine(0)

        return carry

    lax.fori_loop(0, 8, second_chunk, 0)
    combine(1)
    temporal(0)
    temporal(1)
    finish(0)
    finish(1)

    fresh_copy.wait()
    for c in st1 + halos + wave1 + wave2 + wave3 + st2 + q_sends:
        c.wait_send()
    for h in (0, 1):
        q_copy(2, h, z_peers[1], src=1).wait_send()
        for s in (1, 2, 3):
            for c in part_copies(s, h, z_back[s]):
                c.wait_send()
            unit_copy(s, h).wait_send()
            back_copy(s, h, f).wait_send()


def deliver(out_in, fresh_in, out, fresh, held_out, held_fresh, sems):
    steps = []
    for i in range(PARTS):
        rows = pl.ds(i * (T // PARTS), T // PARTS)
        for k, (src, held, dst) in enumerate(((out_in, held_out, out), (fresh_in, held_fresh, fresh))):
            steps.append(
                (
                    pltpu.make_async_copy(src.at[rows], held.at[rows], sems.at[k, i]),
                    pltpu.make_async_copy(held.at[rows], dst.at[rows], sems.at[2 + k, i]),
                )
            )
    for load, _ in steps:
        load.start()
    for load, store in steps:
        load.wait()
        store.start()
    for _, store in steps:
        store.wait()


def codes():
    halves = np.arange(C // 2, dtype=np.float64)
    freqs = np.exp(-math.log(10000.0) * 2.0 * halves / C)
    angles = np.arange(FRAMES)[:, None] * freqs[None, :]
    table = np.stack([np.sin(angles), np.cos(angles)], axis=-1).reshape(FRAMES, C)
    return np.concatenate([table, np.zeros((8 - FRAMES, C))]).astype(np.float32)


def shards(
    latent, gn_gain, gn_bias, conv_weight, w_query, w_kv, w_out, stale_kv, ln_gain, ln_bias, t_query, t_kv, t_out
):
    group = np.arange(C) // (C // GROUPS)
    gmat = jnp.asarray((group[:, None] == group[None, :]).astype(np.float32), BF)
    head = (np.arange(C)[:, None] // THEAD == np.arange(128)[None, :]).astype(np.float32)
    hsum = jnp.asarray(np.concatenate([head, head]), BF)
    hexp = jnp.asarray(head.T.copy(), BF)
    hbm = pl.BlockSpec(memory_space=pl.ANY)
    vmem = pl.BlockSpec(memory_space=pltpu.VMEM)
    dma = pltpu.SemaphoreType.DMA
    out, fresh = pl.pallas_call(
        kernel,
        out_shape=(jax.ShapeDtypeStruct((T, C), F32), jax.ShapeDtypeStruct((T, 2 * HC), BF)),
        in_specs=[hbm] * 9 + [vmem] * 5 + [hbm] * 3,
        out_specs=(vmem, hbm),
        scratch_shapes=[
            pltpu.VMEM((T, C), BF),
            pltpu.VMEM((2, W, C), BF),
            pltpu.VMEM((3, 3 * C, C), BF),
            pltpu.VMEM((C, 3 * HC), BF),
            pltpu.VMEM((HC, C), BF),
            pltpu.VMEM((C, 3 * C), BF),
            pltpu.VMEM((C, C), BF),
            pltpu.VMEM((C, C), BF),
            pltpu.VMEM((4 * W, 3 * C), BF),
            pltpu.VMEM((T, C), F32),
            pltpu.VMEM((T, C), BF),
            pltpu.VMEM((8, 2, C), F32),
            pltpu.VMEM((4, 2, C), F32),
            pltpu.VMEM((4, T, HC), BF),
            pltpu.VMEM((9 * T, 2 * HC), BF),
            pltpu.VMEM((4, HEADS // 2, T, 128), F32),
            pltpu.VMEM((4, HEADS, T, 128), F32),
            pltpu.VMEM((4, HEADS, T, 128), F32),
            pltpu.VMEM((4, T, HC), BF),
            pltpu.VMEM((4, T, HC), BF),
            pltpu.VMEM((4, 2, 8, LSE), F32),
            pltpu.VMEM((4, 2, 8, LSE), F32),
            pltpu.VMEM((T, C), BF),
            pltpu.VMEM((T, C), BF),
            pltpu.VMEM((2, 4, QTR, C), BF),
            pltpu.VMEM((T, C), BF),
            pltpu.VMEM((2 * C, 128), BF),
            pltpu.VMEM((128, C), BF),
            dma((13,)), dma((2,)), dma((2,)), dma((7,)), dma((7,)), dma((3,)), dma((3,)),
            dma((13,)), dma((13,)), dma((6,)), dma((6,)), dma((8,)), dma((8,)), dma((8,)), dma((8,)),
            dma((6,)), dma((6,)), dma((6,)), dma((6,)),
        ],
        compiler_params=pltpu.CompilerParams(
            collective_id=0, has_side_effects=True, vmem_limit_bytes=63 * 2**20
        ),
    )(
        latent.reshape(T, C),
        stale_kv.reshape(T, 2 * HC),
        conv_weight.reshape(3, 3 * C, C),
        w_query,
        w_kv,
        w_out,
        t_query,
        t_kv,
        t_out,
        gn_gain,
        gn_bias,
        ln_gain,
        ln_bias,
        jnp.asarray(codes()),
        gmat,
        hsum,
        hexp,
    )
    out, fresh = pl.pallas_call(
        deliver,
        out_shape=(jax.ShapeDtypeStruct((T, C), F32), jax.ShapeDtypeStruct((T, 2 * HC), BF)),
        in_specs=[hbm] * 2,
        out_specs=(hbm, hbm),
        scratch_shapes=[pltpu.VMEM((T, C), F32), pltpu.VMEM((T, 2 * HC), BF), dma((4, PARTS))],
    )(out, fresh)
    return out.reshape(1, 2, W, C), fresh.reshape(1, 2, W, 2 * HC)


def solution(mesh):
    sharded = P("frame", "patch", None, None)
    placed = (sharded,) + (P(),) * 6 + (sharded,) + (P(),) * 5
    return jax.shard_map(
        shards, mesh=mesh, in_specs=placed, out_specs=(sharded, sharded), check_vma=False
    )
```
